256 devices in a mesh: inst: 16 (over z, x_hi), tp: 16 (over x_lo, y, core).
Axes of the slice: x: 4 (x_hi: 2, x_lo: 2; x = x_hi * 2 + x_lo), y: 4, z: 8, core: 2. Of those that a mesh axis runs over, the one named last changes fastest.
Arguments:
- query: bfloat16 [2, 768, 4096], P(None, 'inst', 'tp'), may hold values from -200 to 200
- new_kv: bfloat16 [2, 768, 2, 1024], P(None, 'inst'), may hold values from -7 to 7
- residual: bfloat16 [2, 768, 8192], P(None, 'inst', 'tp'), may hold values from -60 to 60
- kv_pages: bfloat16 [2304, 2, 16, 128, 128], P('inst', None, 'tp'), may hold values from -6 to 6, as said below
- block_table: int32 [768, 3], P('inst'), may hold values from 0 to 143, as said below
- blocks: int32 [768], P('inst'), may hold values from 1 to 3
- moves: int32 [16, 16], P('inst'), may hold values from 0 to 47, as said below
- out_weight: bfloat16 [4096, 8192], P('tp'), may hold values from -0.5 to 0.5
- norm_gain: bfloat16 [8192], replicated, may hold values from 0.5 to 1.5
Outputs:
- hidden_out: bfloat16 [2, 768, 8192], P(None, 'inst', 'tp')
- normed: bfloat16 [2, 768, 8192], P(None, 'inst')
- arrived_pages: bfloat16 [256, 3, 2, 16, 128, 128], P('inst', None, None, 'tp')
- arrived_tail: bfloat16 [256, 2, 2, 16, 128], P('inst', None, None, 'tp')
The draws below stay inside these ranges and needn't reach their ends.
Inputs may be any that keep to these rules, and one draw needn't show every extreme that they name: `kv_pages`: stored heads a and a2 hold the same numbers whenever a // 2 equals a2 // 2. `block_table`: the 48 x 3 entries of one instance's rows are different pages of its pool. `moves`: the 16 slots in each row are different.
All inputs are finite; a program needn't handle non-finite values.
Results may differ from the reference program's by a relative error of at most 0.0054.
Values may be sent and summed in bfloat16 or wider, within the bound.
No kernel may reach another device: no remote copies, remote signals or barrier semaphores. Data moves between devices by JAX's collectives and lax.ppermute only.
A program may use at most 128 MiB of HBM per device.

```python
import jax
import jax.numpy as jnp
from jax import lax

D = 8192
QH = 32
KVH = 8
HD = 128
PAGE = 128
STEPS = 2
SLOTS = 48
MAXB = 3
INSTANCES = 16
ROWS = 768
POOL = 144
PAGES_ALL = 2304
KVS = 16


def table_of(key):
    base_key = jax.random.fold_in(key, 11)

    def one_instance(index):
        return jax.random.permutation(jax.random.fold_in(base_key, index), POOL).reshape(SLOTS, MAXB)
    tables = jax.vmap(one_instance)(jnp.arange(INSTANCES))
    return tables.reshape(ROWS, MAXB).astype(jnp.int32)


def page_key(key, global_page):
    return jax.random.fold_in(jax.random.fold_in(key, 12), global_page)


def page_of(key, global_page):
    own_key = page_key(key, global_page)
    leading = jax.random.truncated_normal(jax.random.fold_in(own_key, 0), -6.0, 6.0, (2, KVH, 1, HD), jnp.float32)
    others = jax.random.truncated_normal(jax.random.fold_in(own_key, 1), -6.0, 6.0, (2, KVH, PAGE - 1, HD), jnp.float32)
    full_page = jnp.concatenate([leading, others], axis=2)
    return jnp.repeat(full_page, KVS // KVH, axis=1).astype(jnp.bfloat16)


def draw_kv_pages(key, part):
    return lax.map(lambda page_index: page_of(key, page_index), jnp.arange(PAGES_ALL))


def draw_block_table(key, part):
    return table_of(key)


def draw_query(key, part):
    own_key = jax.random.fold_in(key, 21)
    values = jax.random.truncated_normal(own_key, -6.0, 6.0, (STEPS, ROWS, QH * HD), jnp.float32)
    return values.astype(jnp.bfloat16)


def draw_new_kv(key, part):
    own_key = jax.random.fold_in(key, 31)
    values = jax.random.truncated_normal(own_key, -6.0, 6.0, (STEPS, ROWS, 2, KVH * HD), jnp.float32)
    return values.astype(jnp.bfloat16)


def draw_residual(key, part):
    own_key = jax.random.fold_in(key, 41)
    values = jax.random.truncated_normal(own_key, -6.0, 6.0, (STEPS, ROWS, D), jnp.float32)
    rising = 3.0 ** (jnp.arange(D, dtype=jnp.float32) / (D - 1))
    rough = jax.random.uniform(jax.random.fold_in(own_key, 1), (D,), jnp.float32, 0.5, 1.5)
    return (values * rising * rough).astype(jnp.bfloat16)


def draw_moves(key, part):
    own_key = jax.random.fold_in(key, 51)

    def one_instance(index):
        return jax.random.permutation(jax.random.fold_in(own_key, index), SLOTS)[:INSTANCES]
    return jax.vmap(one_instance)(jnp.arange(INSTANCES)).astype(jnp.int32)


def place_ends(values, stream_key, smallest, largest):
    place = [jax.random.randint(jax.random.fold_in(stream_key, axis), (), 0, length) for axis, length in enumerate(values.shape)]
    longest = values.shape.index(max(values.shape))
    neighbour = place[:longest] + [(place[longest] + 1) % values.shape[longest]] + place[longest + 1:]
    return values.at[tuple(place)].set(smallest).at[tuple(neighbour)].set(largest)


def level_of(stream_key, extent, cuts, least, largest):
    level, own = 1.0, jax.random.fold_in(stream_key, 6)
    for axis_at, blocks in cuts:
        steps = jnp.exp(jax.random.uniform(jax.random.fold_in(own, axis_at), (blocks,), jnp.float32, least / len(cuts), largest / len(cuts)))
        level = level * jnp.repeat(steps, extent[axis_at] // blocks).reshape([-1 if axis == axis_at else 1 for axis in range(len(extent))])
    return level


def centred(key, extent, spread, reach, pieces=(), kind=jnp.bfloat16):
    level = level_of(key, extent, pieces, -0.22, 0.18) if pieces else 1.0
    array = jax.random.normal(key, extent, jnp.float32) * spread * level
    return jnp.minimum(jnp.maximum(array, -reach), reach).astype(kind)


def setup_inputs(seed: int = 0) -> dict:
    seeds = jax.random.split(jax.random.key(seed), 10)
    query = draw_query(jax.random.fold_in(seeds[9], 71), 0)
    new_kv = draw_new_kv(jax.random.fold_in(seeds[9], 71), 0)
    residual = draw_residual(jax.random.fold_in(seeds[9], 71), 0)
    kv_pages = draw_kv_pages(jax.random.fold_in(seeds[9], 71), 0)
    block_table = draw_block_table(jax.random.fold_in(seeds[9], 71), 0)
    blocks = place_ends(jax.random.randint(seeds[5], (ROWS,), 1, MAXB + 1), jax.random.fold_in(seeds[5], 1), 1, MAXB).astype(jnp.int32)
    moves = draw_moves(jax.random.fold_in(seeds[9], 71), 0)
    out_weight = centred(seeds[7], (QH * HD, D), HD ** -0.5, 0.5, ((0, 16),))
    norm_gain = jnp.clip(1.0 + 0.1 * jax.random.normal(seeds[8], (D,), jnp.float32), 0.5, 1.5).astype(jnp.bfloat16)
    return {"query": query, "new_kv": new_kv, "residual": residual, "kv_pages": kv_pages, "block_table": block_table, "blocks": blocks, "moves": moves, "out_weight": out_weight, "norm_gain": norm_gain}


epsilon = 1e-05
masked_score = -1e+30

def reference(query, new_kv, residual, kv_pages, block_table, blocks, moves, out_weight, norm_gain):
    group_size = QH // KVS
    copy_count = KVS // KVH
    scaling = HD ** (-0.5)
    pool_view = kv_pages.reshape(INSTANCES, POOL, 2, KVS, PAGE, HD)
    query_view = query.reshape(STEPS, INSTANCES, SLOTS, KVS, group_size, HD).transpose(1, 0, 2, 3, 4, 5)
    fresh_view = new_kv.reshape(STEPS, INSTANCES, SLOTS, 2, KVH, HD)
    head_index = (jnp.arange(KVS) // copy_count).astype(jnp.int32)
    fresh_view = jnp.take(fresh_view, head_index, axis=4).transpose(1, 0, 2, 3, 4, 5)
    table_view = block_table.reshape(INSTANCES, SLOTS, MAXB)
    length_view = blocks.reshape(INSTANCES, SLOTS)

    def attend_instance(packed):
        pool_part, query_part, fresh_part, table_part, length_part = packed
        cached = jnp.take(pool_part, table_part.reshape(-1), axis=0)
        cached = cached.reshape(SLOTS, MAXB, 2, KVS, PAGE, HD).astype(jnp.float32)
        queries = query_part.astype(jnp.float32)
        fresh_keys = fresh_part.astype(jnp.float32)
        cache_scores = jnp.einsum('tsagd,sbapd->tsagbp', queries, cached[:, :, 0]) * scaling
        cache_scores = cache_scores.reshape(STEPS, SLOTS, KVS, group_size, MAXB * PAGE)
        valid = (jnp.arange(MAXB * PAGE) // PAGE)[None, :] < length_part[:, None]
        cache_scores = jnp.where(valid[None, :, None, None, :], cache_scores, masked_score)
        fresh_scores = jnp.einsum('tsagd,usad->tsagu', queries, fresh_keys[:, :, 0]) * scaling
        causal = jnp.arange(STEPS)[None, :] <= jnp.arange(STEPS)[:, None]
        fresh_scores = jnp.where(causal[:, None, None, None, :], fresh_scores, masked_score)
        scores = jnp.concatenate([cache_scores, fresh_scores], axis=-1)
        highest = lax.optimization_barrier(jnp.max(scores, axis=-1, keepdims=True))
        expanded = jnp.exp(scores - highest)
        weights = (expanded / lax.optimization_barrier(jnp.sum(expanded, axis=-1, keepdims=True))).astype(jnp.bfloat16)
        weights = lax.optimization_barrier(weights).astype(jnp.float32)
        cache_weights = weights[..., :MAXB * PAGE].reshape(STEPS, SLOTS, KVS, group_size, MAXB, PAGE)
        mixed = jnp.einsum('tsagbp,sbapd->tsagd', cache_weights, cached[:, :, 1])
        mixed = mixed + jnp.einsum('tsagu,usad->tsagd', weights[..., MAXB * PAGE:], fresh_keys[:, :, 1])
        return mixed.astype(jnp.bfloat16).reshape(STEPS, SLOTS, QH * HD)
    heads = lax.map(attend_instance, (pool_view, query_view, fresh_view, table_view, length_view))
    heads = heads.transpose(1, 0, 2, 3).reshape(STEPS * ROWS, QH * HD)
    attn = jnp.dot(heads, out_weight, preferred_element_type=jnp.float32).reshape(STEPS, ROWS, D)
    hidden_out = (residual.astype(jnp.float32) + attn).astype(jnp.bfloat16)
    hidden_wide = lax.optimization_barrier(hidden_out).astype(jnp.float32)
    mean_square = lax.optimization_barrier(jnp.mean(hidden_wide * hidden_wide, axis=-1, keepdims=True))
    normed = (hidden_wide * lax.rsqrt(mean_square + epsilon) * norm_gain.astype(jnp.float32)).astype(jnp.bfloat16)

    def send_instance(packed):
        pool_part, fresh_part, table_part, length_part, chosen = packed
        page_ids = jnp.take(table_part, chosen, axis=0)
        keep = jnp.arange(MAXB)[None, :] < jnp.take(length_part, chosen)[:, None]
        moved = jnp.take(pool_part, page_ids.reshape(-1), axis=0).reshape(INSTANCES, MAXB, 2, KVS, PAGE, HD)
        moved = jnp.where(keep[:, :, None, None, None, None], moved, jnp.zeros((), moved.dtype))
        tail_rows = jnp.take(fresh_part, chosen, axis=1).transpose(1, 0, 2, 3, 4)
        return (moved, tail_rows)
    sent_pages, sent_tail = lax.map(send_instance, (pool_view, fresh_view, table_view, length_view, moves))
    arrived_pages = sent_pages.transpose(1, 0, 2, 3, 4, 5, 6).reshape(INSTANCES * INSTANCES, MAXB, 2, KVS, PAGE, HD)
    arrived_tail = sent_tail.transpose(1, 0, 2, 3, 4, 5).reshape(INSTANCES * INSTANCES, STEPS, 2, KVS, HD)
    return (hidden_out, normed, arrived_pages, arrived_tail)
```

```python
import functools

import jax
import jax.numpy as jnp
from jax import lax
from jax.experimental import pallas as pl
from jax.experimental.pallas import tpu as pltpu
from jax.sharding import PartitionSpec as P

F32 = jnp.float32
BF16 = jnp.bfloat16
EPSILON = 1e-05
MASKED = -1e30

SLOTS = 48
MAXB = 3
PAGE = 128
HD = 128
STEPS = 2
INST = 16
CHIPS = 8
ROWS = STEPS * SLOTS
D = 8192
SHARE = 512
PAGES = SLOTS * MAXB
TOK = MAXB * PAGE
MSG = TOK + 16
SHIFTS = [(dx, dy) for dx in range(2) for dy in range(4)]


def any_spec():
    return pl.BlockSpec(memory_space=pl.ANY)


def smem_spec():
    return pl.BlockSpec(memory_space=pltpu.SMEM)


def vmem_spec():
    return pl.BlockSpec(memory_space=pltpu.VMEM)


def pack_kernel(tbl, blk, mv, nkv, kv, out, zeros, fresh, stage32, stage, sems, fsem, ssem):
    tp = lax.axis_index("tp")
    core = lax.rem(tp, 2)
    head = lax.div(tp, 2)
    fcopy = pltpu.make_async_copy(
        nkv.at[:, :, :, pl.ds(pl.multiple_of(head * HD, HD), HD)], fresh, fsem
    )
    fcopy.start()
    zeros[...] = jnp.zeros_like(zeros)
    for j in range(INST):
        m = mv[0, j]
        for b in range(MAXB):
            dst = out.at[j, pl.ds(b * PAGE, PAGE)]
            sem = sems.at[j * MAXB + b]
            valid = b < blk[m]

            @pl.when(valid)
            def _():
                pltpu.make_async_copy(kv.at[tbl[m, b], core, 0], dst, sem).start()

            @pl.when(jnp.logical_not(valid))
            def _():
                pltpu.make_async_copy(zeros, dst, sem).start()

    stage32[...] = jnp.zeros_like(stage32)
    fcopy.wait()
    for j in range(INST):
        m = mv[0, j]
        stage32[j, 0:2] = fresh[0, m].astype(F32)
        stage32[j, 2:4] = fresh[1, m].astype(F32)
    stage[...] = stage32[...].astype(BF16)
    scopy = pltpu.make_async_copy(stage, out.at[:, pl.ds(TOK, 16)], ssem)
    scopy.start()
    for j in range(INST):
        for b in range(MAXB):
            pltpu.make_async_copy(
                zeros, out.at[j, pl.ds(b * PAGE, PAGE)], sems.at[j * MAXB + b]
            ).wait()
    scopy.wait()


def pack(block_table, blocks, moves, new_kv, kv_pages):
    return pl.pallas_call(
        pack_kernel,
        out_shape=jax.ShapeDtypeStruct((INST, MSG, HD), BF16),
        in_specs=[smem_spec()] * 3 + [any_spec()] * 2,
        out_specs=any_spec(),
        scratch_shapes=[
            pltpu.VMEM((PAGE, HD), BF16),
            pltpu.VMEM((STEPS, SLOTS, 2, HD), BF16),
            pltpu.VMEM((INST, 16, HD), F32),
            pltpu.VMEM((INST, 16, HD), BF16),
            pltpu.SemaphoreType.DMA((INST * MAXB,)),
            pltpu.SemaphoreType.DMA,
            pltpu.SemaphoreType.DMA,
        ],
        compiler_params=pltpu.CompilerParams(vmem_limit_bytes=8 << 20),
        cost_estimate=pl.CostEstimate(flops=0, bytes_accessed=4 << 20, transcendentals=0),
        name="pack",
    )(block_table, blocks, moves, new_kv, kv_pages)


def attend_kernel(tbl, blk, q, nkv, kv, w, send, keep, kvb, wb, fresh, qs, ks, sc, ob, sbuf, kbuf,
                  kvsem, wsem, fsem, osem):
    tp = lax.axis_index("tp")
    core = lax.rem(tp, 2)
    chip = lax.div(tp, 2)
    x = lax.div(chip, 4)
    y = lax.rem(chip, 4)
    fcopy = pltpu.make_async_copy(
        nkv.at[:, :, :, pl.ds(pl.multiple_of(chip * HD, HD), HD)], fresh, fsem
    )
    fcopy.start()

    def page_copy(s, b):
        return pltpu.make_async_copy(kv.at[tbl[s, b], :, 0], kvb.at[s * MAXB + b], kvsem.at[s * MAXB + b])

    def start_slot(s, carry):
        for b in range(MAXB):
            valid = b < blk[s]

            @pl.when(valid)
            def _():
                page_copy(s, b).start()

            @pl.when(jnp.logical_not(valid))
            def _():
                kvb[s * MAXB + b, 1] = jnp.zeros((PAGE, HD), BF16)
        return carry

    lax.fori_loop(0, SLOTS, start_slot, 0)

    def owner(k):
        dx, dy = SHIFTS[k % CHIPS]
        other = lax.rem(x + dx, 2) * 4 + lax.rem(y + dy, 4)
        return other * 2 + (1 - core if k < CHIPS else core)

    def w_copy(k):
        return pltpu.make_async_copy(
            w.at[:, pl.ds(pl.multiple_of(owner(k) * SHARE, SHARE), SHARE)], wb.at[k], wsem.at[k]
        )

    for k in range(2 * CHIPS):
        w_copy(k).start()

    for t in range(STEPS):
        for g in range(2):
            qs[pl.ds(t * 2 + g, SLOTS, stride=4), :] = q[t, :, g * HD:(g + 1) * HD].astype(F32)
    fcopy.wait()
    fr = fresh[...].astype(F32)
    for u in range(STEPS):
        for c in range(2):
            val = fr[u, :, c, :]
            for j in range(4):
                ks[u * 2 + c, pl.ds(j, SLOTS, stride=4), :] = val

    scaling = HD ** (-0.5)
    row_a = lax.broadcasted_iota(jnp.int32, (8, TOK), 0) < 4
    block_of = lax.div(lax.broadcasted_iota(jnp.int32, (8, TOK), 1), PAGE)

    def wait_slot(s):
        for b in range(MAXB):
            @pl.when(b < blk[s])
            def _():
                page_copy(s, b).wait()

    def score_pair(p, carry):
        wait_slot(2 * p)
        wait_slot(2 * p + 1)
        rows = pl.ds(pl.multiple_of(p * 8, 8), 8)
        q8 = qs[rows, :].astype(BF16)
        parts = []
        for h in range(2):
            keys = kvb[pl.ds((2 * p + h) * MAXB, MAXB), 0].reshape(TOK, HD)
            parts.append(lax.dot_general(q8, keys, (((1,), (1,)), ((), ())), preferred_element_type=F32))
        s8 = jnp.where(row_a, parts[0], parts[1]) * scaling
        count = jnp.where(row_a, blk[2 * p], blk[2 * p + 1])
        sc[rows, :] = jnp.where(block_of < count, s8, MASKED)
        return carry

    lax.fori_loop(0, SLOTS // 2, score_pair, 0)

    qa = qs[...]
    f0 = jnp.sum(qa * ks[0], axis=-1, keepdims=True) * scaling
    f1 = jnp.sum(qa * ks[2], axis=-1, keepdims=True) * scaling
    late = lax.rem(lax.broadcasted_iota(jnp.int32, (SLOTS * 4, 1), 0), 4) >= 2
    f1 = jnp.where(late, f1, MASKED)
    s = sc[...]
    top = jnp.maximum(jnp.max(s, axis=-1, keepdims=True), jnp.maximum(f0, f1))
    e = jnp.exp(s - top)
    e0 = jnp.exp(f0 - top)
    e1 = jnp.exp(f1 - top)
    total = jnp.sum(e, axis=-1, keepdims=True) + e0 + e1
    sc[...] = e / total
    w0 = (e0 / total).astype(BF16).astype(F32)
    w1 = (e1 / total).astype(BF16).astype(F32)
    ob[...] = w0 * ks[1] + w1 * ks[3]
    row_o = lax.broadcasted_iota(jnp.int32, (8, HD), 0) < 4

    def mix_pair(p, carry):
        rows = pl.ds(pl.multiple_of(p * 8, 8), 8)
        w8 = sc[rows, :].astype(BF16)
        parts = []
        for h in range(2):
            vals = kvb[pl.ds((2 * p + h) * MAXB, MAXB), 1].reshape(TOK, HD)
            parts.append(jnp.dot(w8, vals, preferred_element_type=F32))
        ob[rows, :] += jnp.where(row_o, parts[0], parts[1])
        return carry

    lax.fori_loop(0, SLOTS // 2, mix_pair, 0)

    heads = jnp.concatenate(
        [
            jnp.concatenate([ob[pl.ds(t * 2 + g, SLOTS, stride=4), :] for g in range(2)], axis=1)
            for t in range(STEPS)
        ],
        axis=0,
    ).astype(BF16)

    outs = []
    for k in range(2 * CHIPS):
        w_copy(k).wait()
        part = jnp.dot(heads, wb[k], preferred_element_type=F32)
        i = k % CHIPS
        if k < CHIPS:
            sbuf[i] = part.astype(BF16)
            copy = pltpu.make_async_copy(sbuf.at[i], send.at[i], osem.at[k])
        else:
            kbuf[i] = part
            copy = pltpu.make_async_copy(kbuf.at[i], keep.at[i], osem.at[k])
        copy.start()
        outs.append(copy)
    for copy in outs:
        copy.wait()


def attend(block_table, blocks, query, new_kv, kv_pages, out_weight):
    return pl.pallas_call(
        attend_kernel,
        out_shape=(
            jax.ShapeDtypeStruct((CHIPS, ROWS, SHARE), BF16),
            jax.ShapeDtypeStruct((CHIPS, ROWS, SHARE), F32),
        ),
        in_specs=[smem_spec()] * 2 + [vmem_spec()] + [any_spec()] * 3,
        out_specs=(any_spec(), any_spec()),
        scratch_shapes=[
            pltpu.VMEM((PAGES, 2, PAGE, HD), BF16),
            pltpu.VMEM((2 * CHIPS, 2 * HD, SHARE), BF16),
            pltpu.VMEM((STEPS, SLOTS, 2, HD), BF16),
            pltpu.VMEM((SLOTS * 4, HD), F32),
            pltpu.VMEM((4, SLOTS * 4, HD), F32),
            pltpu.VMEM((SLOTS * 4, TOK), F32),
            pltpu.VMEM((SLOTS * 4, HD), F32),
            pltpu.VMEM((CHIPS, ROWS, SHARE), BF16),
            pltpu.VMEM((CHIPS, ROWS, SHARE), F32),
            pltpu.SemaphoreType.DMA((PAGES,)),
            pltpu.SemaphoreType.DMA((2 * CHIPS,)),
            pltpu.SemaphoreType.DMA,
            pltpu.SemaphoreType.DMA((2 * CHIPS,)),
        ],
        compiler_params=pltpu.CompilerParams(vmem_limit_bytes=32 << 20),
        cost_estimate=pl.CostEstimate(flops=10**9, bytes_accessed=16 << 20, transcendentals=10**5),
        name="attend",
    )(block_table, blocks, query, new_kv, kv_pages, out_weight)


def norm_kernel(gain, *refs):
    mine, other, out = refs[:CHIPS], refs[CHIPS], refs[CHIPS + 1]
    tp = lax.axis_index("tp")
    core = lax.rem(tp, 2)
    chip = lax.div(tp, 2)
    x = lax.div(chip, 4)
    y = lax.rem(chip, 4)
    total = jnp.zeros((ROWS, 1), F32)
    for k in range(CHIPS):
        for h in (mine[k][...], other[k]):
            v = h.astype(F32)
            total = total + jnp.sum(v * v, axis=-1, keepdims=True)
    scale = lax.rsqrt(total / D + EPSILON)
    for k, (dx, dy) in enumerate(SHIFTS):
        chunk = lax.rem(x + dx, 2) * 4 + lax.rem(y + dy, 4)
        for part in range(2):
            v = (mine[k][...] if part == 0 else other[k]).astype(F32)
            place = (2 * chunk + (core if part == 0 else 1 - core)) * SHARE
            at = pl.ds(pl.multiple_of(place, SHARE), SHARE)
            out[:, at] = (v * scale * gain[:, at].astype(F32)).astype(BF16)


def norm(gain, mine, other):
    return pl.pallas_call(
        norm_kernel,
        out_shape=jax.ShapeDtypeStruct((ROWS, D), BF16),
        in_specs=[vmem_spec()] * (CHIPS + 2),
        out_specs=vmem_spec(),
        compiler_params=pltpu.CompilerParams(vmem_limit_bytes=16 << 20),
        cost_estimate=pl.CostEstimate(flops=4 * ROWS * D, bytes_accessed=4 * ROWS * D, transcendentals=0),
        name="norm",
    )(gain.reshape(1, D), *mine, other)


def place_kernel(mine, other, out, sems):
    core = lax.rem(lax.axis_index("tp"), 2)
    copies = []
    for b in range(MAXB):
        at = pl.ds(b * PAGE, PAGE)
        for k, ref in enumerate((mine, other)):
            kv = core if k == 0 else 1 - core
            copies.append(pltpu.make_async_copy(ref.at[:, at], out.at[:, b, kv, 0], sems.at[2 * b + k]))
            copies[-1].start()
    for copy in copies:
        copy.wait()


def place(mine, other):
    return pl.pallas_call(
        place_kernel,
        out_shape=jax.ShapeDtypeStruct((INST, MAXB, 2, 1, PAGE, HD), BF16),
        in_specs=[any_spec()] * 2,
        out_specs=any_spec(),
        scratch_shapes=[pltpu.SemaphoreType.DMA((2 * MAXB,))],
        cost_estimate=pl.CostEstimate(flops=0, bytes_accessed=6 << 20, transcendentals=0),
        name="place",
    )(mine, other)


def tp_perm(dx, dy, dc):
    return [
        (k, ((k // 8) ^ dx) * 8 + ((k // 2 % 4 + dy) % 4) * 2 + ((k % 2) ^ dc)) for k in range(16)
    ]


SWAP = tp_perm(0, 0, 1)


def local(query, new_kv, residual, kv_pages, block_table, blocks, moves, out_weight, norm_gain):
    packed = pack(block_table, blocks, moves, new_kv, kv_pages)
    half = lax.all_to_all(packed, "inst", split_axis=0, concat_axis=0, tiled=True)

    send, keep = attend(block_table, blocks, query, new_kv, kv_pages, out_weight)
    got = lax.ppermute(send, "tp", SWAP)
    sums = [keep[k] + got[k].astype(F32) for k in range(CHIPS)]
    order = [k for k in range(CHIPS - 1, 0, -1)]
    terms = {k: lax.ppermute(sums[k].astype(BF16), "tp", tp_perm(*SHIFTS[k], 0)) for k in order}
    attn = sums[0]
    for k in order:
        attn = attn + terms[k].astype(F32)
    hidden = (residual.astype(F32) + attn.reshape(STEPS, SLOTS, SHARE)).astype(BF16)
    flat = hidden.reshape(ROWS, SHARE)
    mine = [flat] + [
        lax.ppermute(flat, "tp", tp_perm(dx, (4 - dy) % 4, 0)) for dx, dy in SHIFTS[1:]
    ]
    other = lax.ppermute(jnp.stack(mine), "tp", SWAP)
    normed = norm(norm_gain, mine, other).reshape(STEPS, SLOTS, D)

    rest = lax.ppermute(half, "tp", SWAP)
    arrived = place(half, rest)
    tail = half[:, TOK:TOK + 4].reshape(INST, STEPS, 2, 1, HD)
    return (hidden, normed, arrived, tail)


def solution(mesh):
    in_specs = (
        P(None, "inst", "tp"),
        P(None, "inst", None, None),
        P(None, "inst", "tp"),
        P("inst", None, "tp", None, None),
        P("inst", None),
        P("inst"),
        P("inst", None),
        P("tp", None),
        P(),
    )
    out_specs = (
        P(None, "inst", "tp"),
        P(None, "inst", None),
        P("inst", None, None, "tp", None, None),
        P("inst", None, None, "tp", None),
    )
    return jax.shard_map(local, mesh=mesh, in_specs=in_specs, out_specs=out_specs, check_vma=False)
```

```python
import functools

import jax
import jax.numpy as jnp
from jax import lax
from jax.experimental import pallas as pl
from jax.experimental.pallas import tpu as pltpu
from jax.sharding import PartitionSpec as P

F32 = jnp.float32
BF16 = jnp.bfloat16
EPSILON = 1e-05
MASKED = -1e30

SLOTS = 48
MAXB = 3
PAGE = 128
HD = 128
STEPS = 2
INST = 16
CHIPS = 8
ROWS = STEPS * SLOTS
D = 8192
SHARE = 512
PAGES = SLOTS * MAXB
TOK = MAXB * PAGE
MSG = TOK + 16
SHIFTS = [(dx, dy) for dy in range(4) for dx in range(2)]


def any_spec():
    return pl.BlockSpec(memory_space=pl.ANY)


def smem_spec():
    return pl.BlockSpec(memory_space=pltpu.SMEM)


def vmem_spec():
    return pl.BlockSpec(memory_space=pltpu.VMEM)


def pack_kernel(tbl, blk, mv, nkv, kv, out, buf, fresh, stage, sems, fsem, osem):
    tp = lax.axis_index("tp")
    core = lax.rem(tp, 2)
    head = lax.div(tp, 2)
    fcopy = pltpu.make_async_copy(
        nkv.at[:, :, :, pl.ds(pl.multiple_of(head * HD, HD), HD)], fresh, fsem
    )
    fcopy.start()

    def page_copy(j, b, page):
        return pltpu.make_async_copy(
            kv.at[page, core, 0], buf.at[j, pl.ds(b * PAGE, PAGE)], sems.at[j * MAXB + b]
        )

    for j in range(INST):
        for b in range(MAXB):
            page_copy(j, b, tbl[b, mv[0, j]]).start()
    stage[...] = jnp.zeros_like(stage)
    fcopy.wait()
    for j in range(INST):
        m = mv[0, j]
        stage[j, 0:2] = fresh[0, m].astype(F32)
        stage[j, 2:4] = fresh[1, m].astype(F32)
    buf[:, TOK:MSG] = stage[...].astype(BF16)
    for j in range(INST):
        count = blk[mv[0, j]]
        for b in range(MAXB):
            page_copy(j, b, 0).wait()
            if b > 0:
                @pl.when(b >= count)
                def _():
                    buf[j, b * PAGE:(b + 1) * PAGE] = jnp.zeros((PAGE, HD), BF16)
    ocopy = pltpu.make_async_copy(buf, out, osem)
    ocopy.start()
    ocopy.wait()


def pack(table, blocks, moves, new_kv, kv_pages):
    return pl.pallas_call(
        pack_kernel,
        out_shape=jax.ShapeDtypeStruct((INST, MSG, HD), BF16),
        in_specs=[smem_spec()] * 3 + [any_spec()] * 2,
        out_specs=any_spec(),
        scratch_shapes=[
            pltpu.VMEM((INST, MSG, HD), BF16),
            pltpu.VMEM((STEPS, SLOTS, 2, HD), BF16),
            pltpu.VMEM((INST, 16, HD), F32),
            pltpu.SemaphoreType.DMA((INST * MAXB,)),
            pltpu.SemaphoreType.DMA,
            pltpu.SemaphoreType.DMA,
        ],
        compiler_params=pltpu.CompilerParams(vmem_limit_bytes=60 << 20),
        cost_estimate=pl.CostEstimate(flops=0, bytes_accessed=4 << 20, transcendentals=0),
        name="pack",
    )(table, blocks, moves, new_kv, kv_pages)


def attend_kernel(tbl, blk, q_hbm, nkv, kv, w, send, keep, kvb, wb, fresh, qs, ks, sc, ob, sbuf, kbuf,
                  kvsem, wsem, fsem, osem, q, qsem):
    qcopy = pltpu.make_async_copy(q_hbm, q, qsem)
    qcopy.start()
    tp = lax.axis_index("tp")
    core = lax.rem(tp, 2)
    chip = lax.div(tp, 2)
    x = lax.div(chip, 4)
    y = lax.rem(chip, 4)
    fcopy = pltpu.make_async_copy(
        nkv.at[:, :, :, pl.ds(pl.multiple_of(chip * HD, HD), HD)], fresh, fsem
    )
    fcopy.start()

    kcopy = pltpu.make_async_copy(kv.at[:, 0, 0], kvb.at[0], kvsem.at[0])
    vcopy = pltpu.make_async_copy(kv.at[:, 1, 0], kvb.at[1], kvsem.at[1])
    kcopy.start()
    vcopy.start()

    def owner(k):
        dx, dy = SHIFTS[k % CHIPS]
        other = lax.rem(x + dx, 2) * 4 + lax.rem(y + dy, 4)
        return other * 2 + (1 - core if k < CHIPS else core)

    wcopy = pltpu.make_async_copy(w, wb, wsem.at[0])
    wcopy.start()

    qcopy.wait()
    for t in range(STEPS):
        for g in range(2):
            qs[pl.ds(t * 2 + g, SLOTS, stride=4), :] = q[t, :, g * HD:(g + 1) * HD].astype(F32)
    fcopy.wait()
    fr = fresh[...].astype(F32)
    for u in range(STEPS):
        for c in range(2):
            val = fr[u, :, c, :]
            for j in range(4):
                ks[u * 2 + c, pl.ds(j, SLOTS, stride=4), :] = val

    scaling = HD ** (-0.5)
    row_a = lax.broadcasted_iota(jnp.int32, (8, TOK), 0) < 4
    block_of = lax.div(lax.broadcasted_iota(jnp.int32, (8, TOK), 1), PAGE)

    def score_pair(p, carry):
        rows = pl.ds(pl.multiple_of(p * 8, 8), 8)
        q8 = qs[rows, :].astype(BF16)
        parts = []
        for h in range(2):
            keys = jnp.concatenate([kvb[0, tbl[b, 2 * p + h]] for b in range(MAXB)], axis=0)
            parts.append(lax.dot_general(q8, keys, (((1,), (1,)), ((), ())), preferred_element_type=F32))
        s8 = jnp.where(row_a, parts[0], parts[1]) * scaling
        count = jnp.where(row_a, blk[2 * p], blk[2 * p + 1])
        sc[rows, :] = jnp.where(block_of < count, s8, MASKED)
        return carry

    kcopy.wait()
    lax.fori_loop(0, SLOTS // 2, score_pair, 0, unroll=True)

    qa = qs[...]
    f0 = jnp.sum(qa * ks[0], axis=-1, keepdims=True) * scaling
    f1 = jnp.sum(qa * ks[2], axis=-1, keepdims=True) * scaling
    late = lax.rem(lax.broadcasted_iota(jnp.int32, (SLOTS * 4, 1), 0), 4) >= 2
    f1 = jnp.where(late, f1, MASKED)
    s = sc[...]
    top = jnp.maximum(jnp.max(s, axis=-1, keepdims=True), jnp.maximum(f0, f1))
    e = jnp.exp(s - top)
    e0 = jnp.exp(f0 - top)
    e1 = jnp.exp(f1 - top)
    total = jnp.sum(e, axis=-1, keepdims=True) + e0 + e1
    sc[...] = e / total
    w0 = (e0 / total).astype(BF16).astype(F32)
    w1 = (e1 / total).astype(BF16).astype(F32)
    ob[...] = w0 * ks[1] + w1 * ks[3]
    row_o = lax.broadcasted_iota(jnp.int32, (8, HD), 0) < 4

    def mix_pair(p, carry):
        rows = pl.ds(pl.multiple_of(p * 8, 8), 8)
        w8 = sc[rows, :].astype(BF16)
        parts = []
        for h in range(2):
            vals = jnp.concatenate([kvb[1, tbl[b, 2 * p + h]] for b in range(MAXB)], axis=0)
            parts.append(jnp.dot(w8, vals, preferred_element_type=F32))
        ob[rows, :] += jnp.where(row_o, parts[0], parts[1])
        return carry

    vcopy.wait()
    lax.fori_loop(0, SLOTS // 2, mix_pair, 0, unroll=True)

    heads = jnp.concatenate(
        [
            jnp.concatenate([ob[pl.ds(t * 2 + g, SLOTS, stride=4), :] for g in range(2)], axis=1)
            for t in range(STEPS)
        ],
        axis=0,
    ).astype(BF16)

    outs = []
    wcopy.wait()
    for k in range(2 * CHIPS):
        cols = pl.ds(pl.multiple_of(owner(k) * SHARE, SHARE), SHARE)
        part = jnp.dot(heads, wb[:, cols], preferred_element_type=F32)
        i = k % CHIPS
        if k < CHIPS:
            sbuf[i] = part.astype(BF16)
            copy = pltpu.make_async_copy(sbuf.at[i], send.at[i], osem.at[k])
        else:
            kbuf[i] = part
            copy = pltpu.make_async_copy(kbuf.at[i], keep.at[i], osem.at[k])
        copy.start()
        outs.append(copy)
    for copy in outs:
        copy.wait()


def attend(table, blocks, query, new_kv, kv_pages, out_weight):
    return pl.pallas_call(
        attend_kernel,
        out_shape=(
            jax.ShapeDtypeStruct((CHIPS, ROWS, SHARE), BF16),
            jax.ShapeDtypeStruct((CHIPS, ROWS, SHARE), F32),
        ),
        in_specs=[smem_spec()] * 2 + [any_spec()] * 4,
        out_specs=(any_spec(), any_spec()),
        scratch_shapes=[
            pltpu.VMEM((2, PAGES, PAGE, HD), BF16),
            pltpu.VMEM((2 * HD, D), BF16),
            pltpu.VMEM((STEPS, SLOTS, 2, HD), BF16),
            pltpu.VMEM((SLOTS * 4, HD), F32),
            pltpu.VMEM((4, SLOTS * 4, HD), F32),
            pltpu.VMEM((SLOTS * 4, TOK), F32),
            pltpu.VMEM((SLOTS * 4, HD), F32),
            pltpu.VMEM((CHIPS, ROWS, SHARE), BF16),
            pltpu.VMEM((CHIPS, ROWS, SHARE), F32),
            pltpu.SemaphoreType.DMA((2,)),
            pltpu.SemaphoreType.DMA((2 * CHIPS,)),
            pltpu.SemaphoreType.DMA,
            pltpu.SemaphoreType.DMA((2 * CHIPS,)),
            pltpu.VMEM((STEPS, SLOTS, 2 * HD), BF16),
            pltpu.SemaphoreType.DMA,
        ],
        compiler_params=pltpu.CompilerParams(vmem_limit_bytes=60 << 20),
        cost_estimate=pl.CostEstimate(flops=10**9, bytes_accessed=16 << 20, transcendentals=10**5),
        name="attend",
    )(table, blocks, query, new_kv, kv_pages, out_weight)


def norm_kernel(gain, *refs):
    mine, other, out = refs[:4], refs[4:8], refs[8]
    tp = lax.axis_index("tp")
    core = lax.rem(tp, 2)
    chip = lax.div(tp, 2)
    x = lax.div(chip, 4)
    y = lax.rem(chip, 4)
    squares = jnp.zeros((ROWS, SHARE), F32)
    for ref in refs[:8]:
        for dx in range(2):
            v = ref[dx].astype(F32)
            squares = squares + v * v
    scale = lax.rsqrt(jnp.sum(squares, axis=-1, keepdims=True) / D + EPSILON)
    for dy in range(4):
        for dx in range(2):
            chunk = lax.rem(x + dx, 2) * 4 + lax.rem(y + dy, 4)
            for ref, parity in ((mine[dy], core), (other[dy], 1 - core)):
                v = ref[dx].astype(F32)
                at = pl.ds(pl.multiple_of((2 * chunk + parity) * SHARE, SHARE), SHARE)
                out[:, at] = (v * scale * gain[:, at].astype(F32)).astype(BF16)


def norm(gain, mine, other):
    return pl.pallas_call(
        norm_kernel,
        out_shape=jax.ShapeDtypeStruct((ROWS, D), BF16),
        in_specs=[vmem_spec()] * 9,
        out_specs=vmem_spec(),
        compiler_params=pltpu.CompilerParams(vmem_limit_bytes=16 << 20),
        cost_estimate=pl.CostEstimate(flops=4 * ROWS * D, bytes_accessed=4 * ROWS * D, transcendentals=0),
        name="norm",
    )(gain.reshape(1, D), *mine, *other)


def place_kernel(other, *refs):
    src, out, sem = refs[0], refs[-2], refs[-1]
    core = lax.rem(lax.axis_index("tp"), 2)
    half = 1 - core if other else core
    copies = [
        pltpu.make_async_copy(src.at[:, pl.ds(b * PAGE, PAGE)], out.at[:, b, half, 0], sem.at[b])
        for b in range(MAXB)
    ]
    for copy in copies:
        copy.start()
    for copy in copies:
        copy.wait()


def place(src, into=None):
    extra = () if into is None else (into,)
    return pl.pallas_call(
        functools.partial(place_kernel, into is not None),
        out_shape=jax.ShapeDtypeStruct((INST, MAXB, 2, 1, PAGE, HD), BF16),
        in_specs=[vmem_spec()] + [any_spec()] * len(extra),
        out_specs=any_spec(),
        scratch_shapes=[pltpu.SemaphoreType.DMA((MAXB,))],
        input_output_aliases={1: 0} if extra else {},
        compiler_params=pltpu.CompilerParams(vmem_limit_bytes=60 << 20),
        cost_estimate=pl.CostEstimate(flops=0, bytes_accessed=3 << 20, transcendentals=0),
        name="place",
    )(src, *extra)


def tp_perm(dx, dy, dc):
    return [
        (k, ((k // 8) ^ dx) * 8 + ((k // 2 % 4 + dy) % 4) * 2 + ((k % 2) ^ dc)) for k in range(16)
    ]


SWAP = tp_perm(0, 0, 1)
CROSS = tp_perm(1, 0, 0)
AROUND = (2, 1, 3)


def local(query, new_kv, residual, kv_pages, block_table, blocks, moves, out_weight, norm_gain):
    table = block_table.T
    packed = pack(table, blocks, moves, new_kv, kv_pages)
    half = lax.all_to_all(packed, "inst", split_axis=0, concat_axis=0, tiled=True)

    send, keep = attend(table, blocks, query, new_kv, kv_pages, out_weight)
    got = lax.ppermute(send, "tp", SWAP)
    sums = [
        keep[2 * dy:2 * dy + 2] + got[2 * dy:2 * dy + 2].astype(F32) for dy in range(4)
    ]
    terms = [lax.ppermute(sums[dy].astype(BF16), "tp", tp_perm(0, dy, 0)) for dy in AROUND]
    total = sums[0]
    for term in terms:
        total = total + term.astype(F32)
    crossed = lax.ppermute(total[1].astype(BF16), "tp", CROSS)
    attn = total[0] + crossed.astype(F32)
    hidden = (residual.astype(F32) + attn.reshape(STEPS, SLOTS, SHARE)).astype(BF16)
    flat = hidden.reshape(ROWS, SHARE)
    pair = jnp.stack([flat, lax.ppermute(flat, "tp", CROSS)])
    mine = {0: pair}
    for dy in AROUND:
        mine[dy] = lax.ppermute(pair, "tp", tp_perm(0, 4 - dy, 0))
    mine = [mine[dy] for dy in range(4)]
    other = [lax.ppermute(block, "tp", SWAP) for block in mine]
    normed = norm(norm_gain, mine, other).reshape(STEPS, SLOTS, D)

    rest = lax.ppermute(half, "tp", SWAP)
    arrived = place(rest, place(half))
    tail = half[:, TOK:TOK + 4].reshape(INST, STEPS, 2, 1, HD)
    return (hidden, normed, arrived, tail)


def solution(mesh):
    in_specs = (
        P(None, "inst", "tp"),
        P(None, "inst", None, None),
        P(None, "inst", "tp"),
        P("inst", None, "tp", None, None),
        P("inst", None),
        P("inst"),
        P("inst", None),
        P("tp", None),
        P(),
    )
    out_specs = (
        P(None, "inst", "tp"),
        P(None, "inst", None),
        P("inst", None, None, "tp", None, None),
        P("inst", None, None, "tp", None),
    )
    return jax.shard_map(local, mesh=mesh, in_specs=in_specs, out_specs=out_specs, check_vma=False)
```

```python
import functools

import jax
import jax.numpy as jnp
from jax import lax
from jax.experimental import pallas as pl
from jax.experimental.pallas import tpu as pltpu
from jax.sharding import PartitionSpec as P

F32 = jnp.float32
BF16 = jnp.bfloat16
EPSILON = 1e-05
MASKED = -1e30

SLOTS = 48
MAXB = 3
PAGE = 128
HD = 128
STEPS = 2
INST = 16
CHIPS = 8
ROWS = STEPS * SLOTS
D = 8192
SHARE = 512
PAGES = SLOTS * MAXB
TOK = MAXB * PAGE
MSG = TOK + 16
Z = 8
SHIFTS = [(dx, dy) for dy in range(4) for dx in range(2)]


def any_spec():
    return pl.BlockSpec(memory_space=pl.ANY)


def smem_spec():
    return pl.BlockSpec(memory_space=pltpu.SMEM)


def vmem_spec():
    return pl.BlockSpec(memory_space=pltpu.VMEM)


def in_hbm(x):
    return pltpu.with_memory_space_constraint(x, pltpu.HBM)


def in_vmem(x):
    return pltpu.with_memory_space_constraint(x, pltpu.VMEM)


def params(mib):
    return pltpu.CompilerParams(vmem_limit_bytes=mib << 20)


def pack_kernel(tbl, blk, mv, nkv, kv, near, far, fresh, stage, sems, fsem):
    tp = lax.axis_index("tp")
    core = lax.rem(tp, 2)
    side = lax.rem(lax.axis_index("inst"), 2)
    fcopy = pltpu.make_async_copy(
        nkv.at[:, :, :, pl.ds(pl.multiple_of(lax.div(tp, 2) * HD, HD), HD)], fresh, fsem
    )
    fcopy.start()

    def page_copy(out, i, z, b, page):
        return pltpu.make_async_copy(
            kv.at[page, core, 0], out.at[z, pl.ds(b * PAGE, PAGE)], sems.at[(i * Z + z) * MAXB + b]
        )

    groups = [
        (out, i, z, mv[0, 2 * z + (side if i == 0 else 1 - side)])
        for i, out in enumerate((near, far))
        for z in range(Z)
    ]
    for out, i, z, m in groups:
        for b in range(MAXB):
            page_copy(out, i, z, b, tbl[b, m]).start()
    stage[...] = jnp.zeros_like(stage)
    fcopy.wait()
    for out, i, z, m in groups:
        stage[i, z, 0:2] = fresh[0, m].astype(F32)
        stage[i, z, 2:4] = fresh[1, m].astype(F32)
    near[:, TOK:MSG] = stage[0].astype(BF16)
    far[:, TOK:MSG] = stage[1].astype(BF16)
    for out, i, z, m in groups:
        count = blk[m]
        for b in range(MAXB):
            page_copy(out, i, z, b, 0).wait()
            if b > 0:
                @pl.when(b >= count)
                def _():
                    out[z, b * PAGE:(b + 1) * PAGE] = jnp.zeros((PAGE, HD), BF16)


def pack(table, blocks, moves, new_kv, kv_pages):
    return pl.pallas_call(
        pack_kernel,
        out_shape=(pltpu.VMEM((Z, MSG, HD), BF16),) * 2,
        in_specs=[smem_spec()] * 3 + [any_spec()] * 2,
        out_specs=(vmem_spec(),) * 2,
        scratch_shapes=[
            pltpu.VMEM((STEPS, SLOTS, 2, HD), BF16),
            pltpu.VMEM((2, Z, 16, HD), F32),
            pltpu.SemaphoreType.DMA((2 * Z * MAXB,)),
            pltpu.SemaphoreType.DMA,
        ],
        compiler_params=params(16),
        cost_estimate=pl.CostEstimate(flops=0, bytes_accessed=4 << 20, transcendentals=0),
        name="pack",
    )(in_hbm(table), in_hbm(blocks), in_hbm(moves), in_hbm(new_kv), in_hbm(kv_pages))


def place_of(tp):
    chip = lax.div(tp, 2)
    return lax.rem(tp, 2), lax.div(chip, 4), lax.rem(chip, 4)


def block_of(x, y, k, parity):
    dx, dy = SHIFTS[k]
    return (lax.rem(x + dx, 2) * 4 + lax.rem(y + dy, 4)) * 2 + parity


def attend_kernel(tbl, blk, q_hbm, nkv, kv, w, send, heads, wb, kvb, fresh, qs, ks, sc, ob, q, kvsem, wsem, fsem, qsem):
    tp = lax.axis_index("tp")
    core, x, y = place_of(tp)
    qcopy = pltpu.make_async_copy(q_hbm, q, qsem)
    qcopy.start()
    fcopy = pltpu.make_async_copy(
        nkv.at[:, :, :, pl.ds(pl.multiple_of(lax.div(tp, 2) * HD, HD), HD)], fresh, fsem
    )
    fcopy.start()
    pools = [pltpu.make_async_copy(kv.at[:, i, 0], kvb.at[i], kvsem.at[i]) for i in range(2)]
    for copy in pools:
        copy.start()
    wcopy = pltpu.make_async_copy(w, wb, wsem)
    wcopy.start()
    qcopy.wait()
    for t in range(STEPS):
        for g in range(2):
            qs[pl.ds(t * 2 + g, SLOTS, stride=4), :] = q[t, :, g * HD:(g + 1) * HD].astype(F32)
    fcopy.wait()
    fr = fresh[...].astype(F32)
    for u in range(STEPS):
        for c in range(2):
            val = fr[u, :, c, :]
            for j in range(4):
                ks[u * 2 + c, pl.ds(j, SLOTS, stride=4), :] = val

    scaling = HD ** (-0.5)
    row_a = lax.broadcasted_iota(jnp.int32, (8, TOK), 0) < 4
    block_no = lax.div(lax.broadcasted_iota(jnp.int32, (8, TOK), 1), PAGE)

    def score_pair(p, carry):
        rows = pl.ds(pl.multiple_of(p * 8, 8), 8)
        q8 = qs[rows, :].astype(BF16)
        parts = []
        for h in range(2):
            keys = jnp.concatenate([kvb[0, tbl[b, 2 * p + h]] for b in range(MAXB)], axis=0)
            parts.append(lax.dot_general(q8, keys, (((1,), (1,)), ((), ())), preferred_element_type=F32))
        s8 = jnp.where(row_a, parts[0], parts[1]) * scaling
        count = jnp.where(row_a, blk[2 * p], blk[2 * p + 1])
        sc[rows, :] = jnp.where(block_no < count, s8, MASKED)
        return carry

    pools[0].wait()
    lax.fori_loop(0, SLOTS // 2, score_pair, 0, unroll=True)

    qa = qs[...]
    f0 = jnp.sum(qa * ks[0], axis=-1, keepdims=True) * scaling
    f1 = jnp.sum(qa * ks[2], axis=-1, keepdims=True) * scaling
    late = lax.rem(lax.broadcasted_iota(jnp.int32, (SLOTS * 4, 1), 0), 4) >= 2
    f1 = jnp.where(late, f1, MASKED)
    s = sc[...]
    top = jnp.maximum(jnp.max(s, axis=-1, keepdims=True), jnp.maximum(f0, f1))
    e = jnp.exp(s - top)
    e0 = jnp.exp(f0 - top)
    e1 = jnp.exp(f1 - top)
    total = jnp.sum(e, axis=-1, keepdims=True) + e0 + e1
    sc[...] = e / total
    w0 = (e0 / total).astype(BF16).astype(F32)
    w1 = (e1 / total).astype(BF16).astype(F32)
    ob[...] = w0 * ks[1] + w1 * ks[3]
    row_o = lax.broadcasted_iota(jnp.int32, (8, HD), 0) < 4

    def mix_pair(p, carry):
        rows = pl.ds(pl.multiple_of(p * 8, 8), 8)
        w8 = sc[rows, :].astype(BF16)
        parts = []
        for h in range(2):
            vals = jnp.concatenate([kvb[1, tbl[b, 2 * p + h]] for b in range(MAXB)], axis=0)
            parts.append(jnp.dot(w8, vals, preferred_element_type=F32))
        ob[rows, :] += jnp.where(row_o, parts[0], parts[1])
        return carry

    pools[1].wait()
    lax.fori_loop(0, SLOTS // 2, mix_pair, 0, unroll=True)

    for t in range(STEPS):
        for g in range(2):
            heads[t * SLOTS:(t + 1) * SLOTS, g * HD:(g + 1) * HD] = ob[
                pl.ds(t * 2 + g, SLOTS, stride=4), :
            ].astype(BF16)
    wcopy.wait()
    project(heads, wb, send, x, y, 1 - core)


def project(heads, wb, out, x, y, parity):
    rows = heads[...]
    for k in range(CHIPS):
        cols = pl.ds(pl.multiple_of(block_of(x, y, k, parity) * SHARE, SHARE), SHARE)
        out[k] = jnp.dot(rows, wb[:, cols], preferred_element_type=F32).astype(out.dtype)


def attend(table, blocks, query, new_kv, kv_pages, out_weight):
    return pl.pallas_call(
        attend_kernel,
        out_shape=(
            pltpu.VMEM((CHIPS, ROWS, SHARE), BF16),
            pltpu.VMEM((ROWS, 2 * HD), BF16),
            pltpu.VMEM((2 * HD, D), BF16),
        ),
        in_specs=[smem_spec()] * 2 + [any_spec()] * 4,
        out_specs=(vmem_spec(),) * 3,
        scratch_shapes=[
            pltpu.VMEM((2, PAGES, PAGE, HD), BF16),
            pltpu.VMEM((STEPS, SLOTS, 2, HD), BF16),
            pltpu.VMEM((SLOTS * 4, HD), F32),
            pltpu.VMEM((4, SLOTS * 4, HD), F32),
            pltpu.VMEM((SLOTS * 4, TOK), F32),
            pltpu.VMEM((SLOTS * 4, HD), F32),
            pltpu.VMEM((STEPS, SLOTS, 2 * HD), BF16),
            pltpu.SemaphoreType.DMA((2,)),
            pltpu.SemaphoreType.DMA,
            pltpu.SemaphoreType.DMA,
            pltpu.SemaphoreType.DMA,
        ],
        compiler_params=params(32),
        cost_estimate=pl.CostEstimate(flops=10**10, bytes_accessed=64 << 20, transcendentals=10**5),
        name="attend",
    )(in_hbm(table), in_hbm(blocks), in_hbm(query), in_hbm(new_kv), in_hbm(kv_pages), in_hbm(out_weight))


def own_kernel(heads, wb, keep):
    core, x, y = place_of(lax.axis_index("tp"))
    project(heads, wb, keep, x, y, core)


def own(heads, wb):
    return pl.pallas_call(
        own_kernel,
        out_shape=pltpu.VMEM((CHIPS, ROWS, SHARE), F32),
        in_specs=[vmem_spec()] * 2,
        out_specs=vmem_spec(),
        compiler_params=params(16),
        cost_estimate=pl.CostEstimate(flops=1, bytes_accessed=1, transcendentals=0),
        name="own",
    )(in_vmem(heads), in_vmem(wb))


def finish_kernel(gain, near, far, far_other, into, *refs):
    blocks, (normed, arrived, tail, buf, sem, nsem) = refs[:8], refs[8:]
    core, x, y = place_of(lax.axis_index("tp"))
    side = lax.rem(lax.axis_index("inst"), 2)
    copies = place_copies(far, far_other, arrived, 1 - side, sem)
    squares = jnp.zeros((ROWS, SHARE), F32)
    for ref in blocks:
        for dx in range(2):
            v = ref[dx].astype(F32)
            squares = squares + v * v
    scale = lax.rsqrt(jnp.sum(squares, axis=-1, keepdims=True) / D + EPSILON)
    for part in range(2):
        for k in range(CHIPS):
            block = block_of(x, y, k, core if part == 0 else 1 - core)
            at = pl.ds(pl.multiple_of(block * SHARE, SHARE), SHARE)
            v = blocks[part * 4 + k // 2][k % 2].astype(F32)
            buf[:, at] = (v * scale * gain[:, at].astype(F32)).astype(BF16)
            copy = pltpu.make_async_copy(buf.at[:, at], normed.at[:, at], nsem.at[part * CHIPS + k])
            copy.start()
            copies.append(copy)
    for refs, way in ((near, side), (far, 1 - side)):
        for z in range(Z):
            tail[2 * z + way] = refs[z, TOK:MSG].astype(F32)[0:4].astype(BF16)
    for copy in copies:
        copy.wait()


def finish(gain, near, far, far_other, into, mine, other):
    return pl.pallas_call(
        finish_kernel,
        out_shape=(
            pltpu.HBM((ROWS, D), BF16),
            pltpu.HBM((INST, MAXB, 2, PAGE, HD), BF16),
            jax.ShapeDtypeStruct((INST, 4, HD), BF16),
        ),
        in_specs=[vmem_spec()] * 4 + [any_spec()] + [vmem_spec()] * 8,
        out_specs=(any_spec(), any_spec(), vmem_spec()),
        scratch_shapes=[
            pltpu.VMEM((ROWS, D), BF16),
            pltpu.SemaphoreType.DMA((2 * Z * MAXB,)),
            pltpu.SemaphoreType.DMA((2 * CHIPS,)),
        ],
        input_output_aliases={4: 1},
        compiler_params=params(24),
        cost_estimate=pl.CostEstimate(flops=4 * ROWS * D, bytes_accessed=8 << 20, transcendentals=0),
        name="finish",
    )(gain.reshape(1, D), near, far, far_other, into, *mine, *other)


def place_copies(mine, other, out, way, sems):
    core = lax.rem(lax.axis_index("tp"), 2)
    copies = []
    for part, (src, half) in enumerate(((mine, core), (other, 1 - core))):
        for z in range(Z):
            for b in range(MAXB):
                copies.append(
                    pltpu.make_async_copy(
                        src.at[z, pl.ds(b * PAGE, PAGE)],
                        out.at[2 * z + way, b, half],
                        sems.at[(part * Z + z) * MAXB + b],
                    )
                )
                copies[-1].start()
    return copies


def place_kernel(mine, other, out, sems):
    side = lax.rem(lax.axis_index("inst"), 2)
    for copy in place_copies(mine, other, out, side, sems):
        copy.wait()


def place(mine, other):
    return pl.pallas_call(
        place_kernel,
        out_shape=pltpu.HBM((INST, MAXB, 2, PAGE, HD), BF16),
        in_specs=[vmem_spec()] * 2,
        out_specs=any_spec(),
        scratch_shapes=[pltpu.SemaphoreType.DMA((2 * Z * MAXB,))],
        compiler_params=params(8),
        cost_estimate=pl.CostEstimate(flops=0, bytes_accessed=3 << 20, transcendentals=0),
        name="place",
    )(mine, other)


def tp_perm(dx, dy, dc):
    return [
        (k, ((k // 8) ^ dx) * 8 + ((k // 2 % 4 + dy) % 4) * 2 + ((k % 2) ^ dc)) for k in range(16)
    ]


SWAP = tp_perm(0, 0, 1)
CROSS = tp_perm(1, 0, 0)
AROUND = (2, 1, 3)


Z_GROUPS = [[2 * z + side for z in range(Z)] for side in range(2)]
SIDES = [(k, k ^ 1) for k in range(INST)]


def along_z(x):
    return lax.all_to_all(x, "inst", 0, 0, tiled=True, axis_index_groups=Z_GROUPS)


def after(x, *values):
    return lax.optimization_barrier((x, *values))[0]


def local(query, new_kv, residual, kv_pages, block_table, blocks, moves, out_weight, norm_gain):
    table = block_table.T
    own_rows = residual.reshape(ROWS, SHARE)
    peer_rows = lax.ppermute(own_rows, "tp", CROSS)
    near, far = pack(table, blocks, moves, new_kv, kv_pages)
    far = lax.ppermute(far, "inst", SIDES)
    near = along_z(near)

    send, heads, weight = attend(table, blocks, query, new_kv, kv_pages, out_weight)
    got = after(lax.ppermute(send, "tp", SWAP), far)
    keep = own(heads, weight)
    sums = [
        keep[2 * dy:2 * dy + 2] + got[2 * dy:2 * dy + 2].astype(F32) for dy in range(4)
    ]
    terms = [lax.ppermute(sums[dy].astype(BF16), "tp", tp_perm(0, dy, 0)) for dy in AROUND]
    terms[0] = after(terms[0], near)
    far = along_z(after(far, sums[1], near))
    total = sums[0]
    for term in terms:
        total = total + term.astype(F32)
    part = total.astype(BF16)
    cross = lax.ppermute(part, "tp", CROSS)
    pair = jnp.stack(
        [
            (rows.astype(F32) + (part[dx].astype(F32) + cross[1 - dx].astype(F32))).astype(BF16)
            for dx, rows in enumerate((own_rows, peer_rows))
        ]
    )
    hidden = pair[0].reshape(STEPS, SLOTS, SHARE)
    mine = {0: pair}
    for dy in AROUND:
        mine[dy] = lax.ppermute(pair, "tp", tp_perm(0, 4 - dy, 0))
    mine = [mine[dy] for dy in range(4)]
    arrived = place(near, lax.ppermute(after(near, part), "tp", SWAP))
    mine[2], arrived = lax.optimization_barrier((mine[2], arrived))
    far = after(far, *mine)
    far_other = lax.ppermute(far, "tp", SWAP)
    other = [lax.ppermute(block, "tp", SWAP) for block in mine]
    normed, arrived, tail = finish(norm_gain, near, far, far_other, arrived, mine, other)
    return (
        hidden,
        normed.reshape(STEPS, SLOTS, D),
        arrived.reshape(INST, MAXB, 2, 1, PAGE, HD),
        tail.reshape(INST, STEPS, 2, 1, HD),
    )


def solution(mesh):
    in_specs = (
        P(None, "inst", "tp"),
        P(None, "inst", None, None),
        P(None, "inst", "tp"),
        P("inst", None, "tp", None, None),
        P("inst", None),
        P("inst"),
        P("inst", None),
        P("tp", None),
        P(),
    )
    out_specs = (
        P(None, "inst", "tp"),
        P(None, "inst", None),
        P("inst", None, None, "tp", None, None),
        P("inst", None, None, "tp", None),
    )
    return jax.shard_map(local, mesh=mesh, in_specs=in_specs, out_specs=out_specs, check_vma=False)
```

```python
import functools

import jax
import jax.numpy as jnp
from jax import lax
from jax.experimental import pallas as pl
from jax.experimental.pallas import tpu as pltpu
from jax.sharding import PartitionSpec as P

F32 = jnp.float32
BF16 = jnp.bfloat16
EPSILON = 1e-05
MASKED = -1e30

SLOTS = 48
MAXB = 3
PAGE = 128
HD = 128
STEPS = 2
INST = 16
CHIPS = 8
ROWS = STEPS * SLOTS
D = 8192
SHARE = 512
PAGES = SLOTS * MAXB
TOK = MAXB * PAGE
MSG = TOK + 16
Z = 8
SHIFTS = [(dx, dy) for dy in range(4) for dx in range(2)]


def any_spec():
    return pl.BlockSpec(memory_space=pl.ANY)


def smem_spec():
    return pl.BlockSpec(memory_space=pltpu.SMEM)


def vmem_spec():
    return pl.BlockSpec(memory_space=pltpu.VMEM)


def in_hbm(x):
    return pltpu.with_memory_space_constraint(x, pltpu.HBM)


def in_vmem(x):
    return pltpu.with_memory_space_constraint(x, pltpu.VMEM)


def params(mib):
    return pltpu.CompilerParams(vmem_limit_bytes=mib << 20)


def pack_kernel(tbl, blk, mv, nkv, kv, near_out, far, near, fresh, stage, sems, fsem, osem):
    tp = lax.axis_index("tp")
    core = lax.rem(tp, 2)
    side = lax.rem(lax.axis_index("inst"), 2)
    fcopy = pltpu.make_async_copy(
        nkv.at[:, :, :, pl.ds(pl.multiple_of(lax.div(tp, 2) * HD, HD), HD)], fresh, fsem
    )
    fcopy.start()

    def page_copy(out, i, z, b, page):
        return pltpu.make_async_copy(
            kv.at[page, core, 0], out.at[z, pl.ds(b * PAGE, PAGE)], sems.at[(i * Z + z) * MAXB + b]
        )

    groups = [
        (out, i, z, mv[0, 2 * z + (side if i == 0 else 1 - side)])
        for i, out in enumerate((near, far))
        for z in range(Z)
    ]
    for out, i, z, m in groups:
        for b in range(MAXB):
            page_copy(out, i, z, b, tbl[b, m]).start()
    stage[...] = jnp.zeros_like(stage)
    fcopy.wait()
    for out, i, z, m in groups:
        stage[i, z, 0:2] = fresh[0, m].astype(F32)
        stage[i, z, 2:4] = fresh[1, m].astype(F32)
    near[:, TOK:MSG] = stage[0].astype(BF16)
    far[:, TOK:MSG] = stage[1].astype(BF16)
    for n, (out, i, z, m) in enumerate(groups):
        count = blk[m]
        if n == Z:
            ocopy = pltpu.make_async_copy(near, near_out, osem)
            ocopy.start()
        for b in range(MAXB):
            page_copy(out, i, z, b, 0).wait()
            if b > 0:
                @pl.when(b >= count)
                def _():
                    out[z, b * PAGE:(b + 1) * PAGE] = jnp.zeros((PAGE, HD), BF16)
    ocopy.wait()


def pack(table, blocks, moves, new_kv, kv_pages):
    return pl.pallas_call(
        pack_kernel,
        out_shape=(pltpu.HBM((Z, MSG, HD), BF16), pltpu.VMEM((Z, MSG, HD), BF16)),
        in_specs=[smem_spec()] * 3 + [any_spec()] * 2,
        out_specs=(any_spec(), vmem_spec()),
        scratch_shapes=[
            pltpu.VMEM((Z, MSG, HD), BF16),
            pltpu.VMEM((STEPS, SLOTS, 2, HD), BF16),
            pltpu.VMEM((2, Z, 16, HD), F32),
            pltpu.SemaphoreType.DMA((2 * Z * MAXB,)),
            pltpu.SemaphoreType.DMA,
            pltpu.SemaphoreType.DMA,
        ],
        compiler_params=params(16),
        cost_estimate=pl.CostEstimate(flops=0, bytes_accessed=4 << 20, transcendentals=0),
        name="pack",
    )(in_hbm(table), in_hbm(blocks), in_hbm(moves), in_hbm(new_kv), in_hbm(kv_pages))


def touch_kernel(x, out):
    del x, out


def touch(x):
    return pl.pallas_call(
        touch_kernel,
        out_shape=pltpu.HBM(x.shape, x.dtype),
        in_specs=[any_spec()],
        out_specs=any_spec(),
        input_output_aliases={0: 0},
        cost_estimate=pl.CostEstimate(flops=0, bytes_accessed=128 << 20, transcendentals=0),
        name="touch",
    )(in_hbm(x))


def place_of(tp):
    chip = lax.div(tp, 2)
    return lax.rem(tp, 2), lax.div(chip, 4), lax.rem(chip, 4)


def block_of(x, y, k, parity):
    dx, dy = SHIFTS[k]
    return (lax.rem(x + dx, 2) * 4 + lax.rem(y + dy, 4)) * 2 + parity


def attend_kernel(tbl, blk, q_hbm, nkv, kv, w, send, heads, wb, kvb, fresh, qs, ks, sc, ob, q, kvsem, wsem, fsem, qsem):
    tp = lax.axis_index("tp")
    core, x, y = place_of(tp)
    qcopy = pltpu.make_async_copy(q_hbm, q, qsem)
    qcopy.start()
    fcopy = pltpu.make_async_copy(
        nkv.at[:, :, :, pl.ds(pl.multiple_of(lax.div(tp, 2) * HD, HD), HD)], fresh, fsem
    )
    fcopy.start()
    pools = [pltpu.make_async_copy(kv.at[:, i, 0], kvb.at[i], kvsem.at[i]) for i in range(2)]
    for copy in pools:
        copy.start()
    wcopy = pltpu.make_async_copy(w, wb, wsem)
    wcopy.start()
    qcopy.wait()
    for t in range(STEPS):
        for g in range(2):
            qs[pl.ds(t * 2 + g, SLOTS, stride=4), :] = q[t, :, g * HD:(g + 1) * HD].astype(F32)
    fcopy.wait()
    fr = fresh[...].astype(F32)
    for u in range(STEPS):
        for c in range(2):
            val = fr[u, :, c, :]
            for j in range(4):
                ks[u * 2 + c, pl.ds(j, SLOTS, stride=4), :] = val

    scaling = HD ** (-0.5)
    row_a = lax.broadcasted_iota(jnp.int32, (8, TOK), 0) < 4
    block_no = lax.div(lax.broadcasted_iota(jnp.int32, (8, TOK), 1), PAGE)

    def score_pair(p, carry):
        rows = pl.ds(pl.multiple_of(p * 8, 8), 8)
        q8 = qs[rows, :].astype(BF16)
        parts = []
        for h in range(2):
            keys = jnp.concatenate([kvb[0, tbl[b, 2 * p + h]] for b in range(MAXB)], axis=0)
            parts.append(lax.dot_general(q8, keys, (((1,), (1,)), ((), ())), preferred_element_type=F32))
        s8 = jnp.where(row_a, parts[0], parts[1]) * scaling
        count = jnp.where(row_a, blk[2 * p], blk[2 * p + 1])
        sc[rows, :] = jnp.where(block_no < count, s8, MASKED)
        return carry

    pools[0].wait()
    lax.fori_loop(0, SLOTS // 2, score_pair, 0, unroll=True)

    qa = qs[...]
    f0 = jnp.sum(qa * ks[0], axis=-1, keepdims=True) * scaling
    f1 = jnp.sum(qa * ks[2], axis=-1, keepdims=True) * scaling
    late = lax.rem(lax.broadcasted_iota(jnp.int32, (SLOTS * 4, 1), 0), 4) >= 2
    f1 = jnp.where(late, f1, MASKED)
    s = sc[...]
    top = jnp.maximum(jnp.max(s, axis=-1, keepdims=True), jnp.maximum(f0, f1))
    e = jnp.exp(s - top)
    e0 = jnp.exp(f0 - top)
    e1 = jnp.exp(f1 - top)
    total = jnp.sum(e, axis=-1, keepdims=True) + e0 + e1
    sc[...] = e / total
    w0 = (e0 / total).astype(BF16).astype(F32)
    w1 = (e1 / total).astype(BF16).astype(F32)
    ob[...] = w0 * ks[1] + w1 * ks[3]
    row_o = lax.broadcasted_iota(jnp.int32, (8, HD), 0) < 4

    def mix_pair(p, carry):
        rows = pl.ds(pl.multiple_of(p * 8, 8), 8)
        w8 = sc[rows, :].astype(BF16)
        parts = []
        for h in range(2):
            vals = jnp.concatenate([kvb[1, tbl[b, 2 * p + h]] for b in range(MAXB)], axis=0)
            parts.append(jnp.dot(w8, vals, preferred_element_type=F32))
        ob[rows, :] += jnp.where(row_o, parts[0], parts[1])
        return carry

    pools[1].wait()
    lax.fori_loop(0, SLOTS // 2, mix_pair, 0, unroll=True)

    for t in range(STEPS):
        for g in range(2):
            heads[t * SLOTS:(t + 1) * SLOTS, g * HD:(g + 1) * HD] = ob[
                pl.ds(t * 2 + g, SLOTS, stride=4), :
            ].astype(BF16)
    wcopy.wait()
    project(heads, wb, send, x, y, 1 - core)


def project(heads, wb, out, x, y, parity):
    rows = heads[...]
    for k in range(CHIPS):
        cols = pl.ds(pl.multiple_of(block_of(x, y, k, parity) * SHARE, SHARE), SHARE)
        out[k] = jnp.dot(rows, wb[:, cols], preferred_element_type=F32).astype(out.dtype)


def attend(table, blocks, query, new_kv, kv_pages, out_weight):
    return pl.pallas_call(
        attend_kernel,
        out_shape=(
            pltpu.VMEM((CHIPS, ROWS, SHARE), BF16),
            pltpu.VMEM((ROWS, 2 * HD), BF16),
            pltpu.VMEM((2 * HD, D), BF16),
        ),
        in_specs=[smem_spec()] * 2 + [any_spec()] * 4,
        out_specs=(vmem_spec(),) * 3,
        scratch_shapes=[
            pltpu.VMEM((2, PAGES, PAGE, HD), BF16),
            pltpu.VMEM((STEPS, SLOTS, 2, HD), BF16),
            pltpu.VMEM((SLOTS * 4, HD), F32),
            pltpu.VMEM((4, SLOTS * 4, HD), F32),
            pltpu.VMEM((SLOTS * 4, TOK), F32),
            pltpu.VMEM((SLOTS * 4, HD), F32),
            pltpu.VMEM((STEPS, SLOTS, 2 * HD), BF16),
            pltpu.SemaphoreType.DMA((2,)),
            pltpu.SemaphoreType.DMA,
            pltpu.SemaphoreType.DMA,
            pltpu.SemaphoreType.DMA,
        ],
        compiler_params=params(32),
        cost_estimate=pl.CostEstimate(flops=10**10, bytes_accessed=64 << 20, transcendentals=10**5),
        name="attend",
    )(in_hbm(table), in_hbm(blocks), in_hbm(query), in_hbm(new_kv), in_hbm(kv_pages), in_hbm(out_weight))


def own_kernel(heads, wb, got, *outs):
    core, x, y = place_of(lax.axis_index("tp"))
    rows = heads[...]
    for k in range(CHIPS):
        cols = pl.ds(pl.multiple_of(block_of(x, y, k, core) * SHARE, SHARE), SHARE)
        part = jnp.dot(rows, wb[:, cols], preferred_element_type=F32) + got[k].astype(F32)
        outs[k // 2][k % 2] = part.astype(outs[k // 2].dtype)


def own(heads, wb, got):
    return pl.pallas_call(
        own_kernel,
        out_shape=tuple(pltpu.VMEM((2, ROWS, SHARE), F32 if dy == 0 else BF16) for dy in range(4)),
        in_specs=[vmem_spec()] * 3,
        out_specs=(vmem_spec(),) * 4,
        compiler_params=params(16),
        cost_estimate=pl.CostEstimate(flops=1, bytes_accessed=1, transcendentals=0),
        name="own",
    )(in_vmem(heads), in_vmem(wb), in_vmem(got))


def norm_kernel(gain, *refs):
    blocks, (normed, buf, nsem) = refs[:8], refs[8:]
    core, x, y = place_of(lax.axis_index("tp"))
    squares = jnp.zeros((ROWS, SHARE), F32)
    for ref in blocks:
        for dx in range(2):
            v = ref[dx].astype(F32)
            squares = squares + v * v
    scale = lax.rsqrt(jnp.sum(squares, axis=-1, keepdims=True) / D + EPSILON)
    copies = []
    for part in range(2):
        for k in range(CHIPS):
            block = block_of(x, y, k, core if part == 0 else 1 - core)
            at = pl.ds(pl.multiple_of(block * SHARE, SHARE), SHARE)
            v = blocks[part * 4 + k // 2][k % 2].astype(F32)
            buf[:, at] = (v * scale * gain[:, at].astype(F32)).astype(BF16)
            copy = pltpu.make_async_copy(buf.at[:, at], normed.at[:, at], nsem.at[part * CHIPS + k])
            copy.start()
            copies.append(copy)
    for copy in copies:
        copy.wait()


def norm(gain, mine, other):
    return pl.pallas_call(
        norm_kernel,
        out_shape=pltpu.HBM((ROWS, D), BF16),
        in_specs=[vmem_spec()] * 9,
        out_specs=any_spec(),
        scratch_shapes=[
            pltpu.VMEM((ROWS, D), BF16),
            pltpu.SemaphoreType.DMA((2 * CHIPS,)),
        ],
        compiler_params=params(24),
        cost_estimate=pl.CostEstimate(flops=4 * ROWS * D, bytes_accessed=8 << 20, transcendentals=0),
        name="norm",
    )(gain.reshape(1, D), *mine, *other)


def half_copies(src, out, way, half, sems, first):
    copies = []
    for z in range(Z):
        for b in range(MAXB):
            copies.append(
                pltpu.make_async_copy(
                    src.at[z, pl.ds(b * PAGE, PAGE)],
                    out.at[2 * z + way, b, half],
                    sems.at[first + z * MAXB + b],
                )
            )
            copies[-1].start()
    return copies


def place_near_kernel(mine, other, out, rows, sems):
    core = lax.rem(lax.axis_index("tp"), 2)
    side = lax.rem(lax.axis_index("inst"), 2)
    copies = half_copies(mine, out, side, core, sems, 0)
    copies += half_copies(other, out, side, 1 - core, sems, Z * MAXB)
    for z in range(Z):
        rows[z] = mine[z, TOK:MSG].astype(F32)[0:4]
    for copy in copies:
        copy.wait()


def place_near(mine, other):
    return pl.pallas_call(
        place_near_kernel,
        out_shape=(
            pltpu.HBM((INST, MAXB, 2, PAGE, HD), BF16),
            jax.ShapeDtypeStruct((Z, 4, HD), F32),
        ),
        in_specs=[vmem_spec()] * 2,
        out_specs=(any_spec(), vmem_spec()),
        scratch_shapes=[pltpu.SemaphoreType.DMA((2 * Z * MAXB,))],
        compiler_params=params(8),
        cost_estimate=pl.CostEstimate(flops=0, bytes_accessed=3 << 20, transcendentals=0),
        name="place_near",
    )(mine, other)


def place_far_kernel(other, src, *refs):
    out, sems = refs[-2:] if other else (refs[-3], refs[-1])
    core = lax.rem(lax.axis_index("tp"), 2)
    side = lax.rem(lax.axis_index("inst"), 2)
    copies = half_copies(src, out, 1 - side, 1 - core if other else core, sems, 0)
    if not other:
        rows, tail = refs[0], refs[-2]
        for z in range(Z):
            tail[2 * z + side] = rows[z].astype(BF16)
            tail[2 * z + 1 - side] = src[z, TOK:MSG].astype(F32)[0:4].astype(BF16)
    for copy in copies:
        copy.wait()


def place_far(src, into, rows=None):
    whole = pltpu.HBM((INST, MAXB, 2, PAGE, HD), BF16)
    own_half = rows is not None
    return pl.pallas_call(
        functools.partial(place_far_kernel, not own_half),
        out_shape=(whole, jax.ShapeDtypeStruct((INST, 4, HD), BF16)) if own_half else whole,
        in_specs=[vmem_spec()] * (2 if own_half else 1) + [any_spec()],
        out_specs=(any_spec(), vmem_spec()) if own_half else any_spec(),
        scratch_shapes=[pltpu.SemaphoreType.DMA((Z * MAXB,))],
        input_output_aliases={2 if own_half else 1: 0},
        compiler_params=params(8),
        cost_estimate=pl.CostEstimate(flops=0, bytes_accessed=3 << 20, transcendentals=0),
        name="place_far",
    )(src, *((rows,) if own_half else ()), into)


def tp_perm(dx, dy, dc):
    return [
        (k, ((k // 8) ^ dx) * 8 + ((k // 2 % 4 + dy) % 4) * 2 + ((k % 2) ^ dc)) for k in range(16)
    ]


SWAP = tp_perm(0, 0, 1)
CROSS = tp_perm(1, 0, 0)
AROUND = (2, 1, 3)


Z_GROUPS = [[2 * z + side for z in range(Z)] for side in range(2)]
SIDES = [(k, k ^ 1) for k in range(INST)]


def along_z(x):
    return lax.all_to_all(x, "inst", 0, 0, tiled=True, axis_index_groups=Z_GROUPS)


def after(x, *values):
    return lax.optimization_barrier((x, *values))[0]


def local(query, new_kv, residual, kv_pages, block_table, blocks, moves, out_weight, norm_gain):
    table = block_table.T
    near, far = pack(table, blocks, moves, new_kv, kv_pages)
    far = lax.ppermute(far, "inst", SIDES)
    near = along_z(touch(near))

    send, heads, weight = attend(table, blocks, query, new_kv, kv_pages, out_weight)
    got = lax.ppermute(send, "tp", SWAP)
    sums = own(after(heads, far), weight, got)
    terms = [lax.ppermute(sums[dy], "tp", tp_perm(0, dy, 0)) for dy in AROUND]
    terms[0] = after(terms[0], near)
    far = along_z(after(far, sums[1]))
    total = sums[0]
    for term in terms:
        total = total + term.astype(F32)
    own_rows = residual.reshape(ROWS, SHARE).astype(F32)
    part = jnp.stack([own_rows + total[0], total[1]]).astype(BF16)
    cross = lax.ppermute(part, "tp", CROSS)
    pair = jnp.stack(
        [(part[dx].astype(F32) + cross[1 - dx].astype(F32)).astype(BF16) for dx in range(2)]
    )
    hidden = pair[0].reshape(STEPS, SLOTS, SHARE)
    mine = {0: pair}
    for dy in AROUND:
        mine[dy] = lax.ppermute(pair, "tp", tp_perm(0, 4 - dy, 0))
    mine = [mine[dy] for dy in range(4)]
    near = after(near, pair)
    arrived, rows = place_near(near, lax.ppermute(near, "tp", SWAP))
    mine[2], arrived, hidden = lax.optimization_barrier((mine[2], arrived, hidden))
    other = [lax.ppermute(block, "tp", SWAP) for block in mine]
    normed = norm(norm_gain, mine, other)
    far = after(far, *mine)
    far_other = lax.ppermute(far, "tp", SWAP)
    arrived, tail = place_far(far, arrived, rows)
    arrived = place_far(far_other, arrived)
    return (
        hidden,
        normed.reshape(STEPS, SLOTS, D),
        arrived.reshape(INST, MAXB, 2, 1, PAGE, HD),
        tail.reshape(INST, STEPS, 2, 1, HD),
    )


def solution(mesh):
    in_specs = (
        P(None, "inst", "tp"),
        P(None, "inst", None, None),
        P(None, "inst", "tp"),
        P("inst", None, "tp", None, None),
        P("inst", None),
        P("inst"),
        P("inst", None),
        P("tp", None),
        P(),
    )
    out_specs = (
        P(None, "inst", "tp"),
        P(None, "inst", None),
        P("inst", None, None, "tp", None, None),
        P("inst", None, None, "tp", None),
    )
    return jax.shard_map(local, mesh=mesh, in_specs=in_specs, out_specs=out_specs, check_vma=False)
```

```python
import functools

import jax
import jax.numpy as jnp
from jax import lax
from jax.experimental import pallas as pl
from jax.experimental.pallas import tpu as pltpu
from jax.sharding import PartitionSpec as P

F32 = jnp.float32
BF16 = jnp.bfloat16
EPSILON = 1e-05
MASKED = -1e30

SLOTS = 48
MAXB = 3
PAGE = 128
HD = 128
STEPS = 2
INST = 16
CHIPS = 8
ROWS = STEPS * SLOTS
D = 8192
SHARE = 512
PAGES = SLOTS * MAXB
TOK = MAXB * PAGE
MSG = TOK + 16
Z = 8
SHIFTS = [(dx, dy) for dy in range(4) for dx in range(2)]


def any_spec():
    return pl.BlockSpec(memory_space=pl.ANY)


def smem_spec():
    return pl.BlockSpec(memory_space=pltpu.SMEM)


def vmem_spec():
    return pl.BlockSpec(memory_space=pltpu.VMEM)


def in_hbm(x):
    return pltpu.with_memory_space_constraint(x, pltpu.HBM)


def in_vmem(x):
    return pltpu.with_memory_space_constraint(x, pltpu.VMEM)


def params(mib):
    return pltpu.CompilerParams(vmem_limit_bytes=mib << 20)


def pack_kernel(far, tbl, blk, mv, nkv, kv, *refs):
    if far:
        buf, fresh, stage, sems, fsem = refs[-5:]
    else:
        out, buf, fresh, stage, sems, fsem, osems = refs
    tp = lax.axis_index("tp")
    core = lax.rem(tp, 2)
    side = lax.rem(lax.axis_index("inst"), 2)
    slots = [mv[0, 2 * z + (1 - side if far else side)] for z in range(Z)]

    def page_copy(z, b, page):
        return pltpu.make_async_copy(
            kv.at[page, core, 0], buf.at[z, pl.ds(b * PAGE, PAGE)], sems.at[z * MAXB + b]
        )

    fcopy = pltpu.make_async_copy(
        nkv.at[:, :, :, pl.ds(pl.multiple_of(lax.div(tp, 2) * HD, HD), HD)], fresh, fsem
    )
    fcopy.start()
    for z, m in enumerate(slots):
        for b in range(MAXB):
            page_copy(z, b, tbl[b, m]).start()
    stage[...] = jnp.zeros_like(stage)
    fcopy.wait()
    for z, m in enumerate(slots):
        stage[z, 0:2] = fresh[0, m].astype(F32)
        stage[z, 2:4] = fresh[1, m].astype(F32)
    buf[:, TOK:MSG] = stage[...].astype(BF16)
    copies = []
    for z, m in enumerate(slots):
        count = blk[m]
        for b in range(MAXB):
            page_copy(z, b, 0).wait()
            if b > 0:
                @pl.when(b >= count)
                def _():
                    buf[z, b * PAGE:(b + 1) * PAGE] = jnp.zeros((PAGE, HD), BF16)
        if not far:
            copies.append(pltpu.make_async_copy(buf.at[z], out.at[z], osems.at[z]))
            copies[-1].start()
    for copy in copies:
        copy.wait()


def pack(far, table, blocks, moves, new_kv, kv_pages, *first):
    shape = (Z, MSG, HD)
    return pl.pallas_call(
        functools.partial(pack_kernel, far),
        out_shape=pltpu.VMEM(shape, BF16) if far else pltpu.HBM(shape, BF16),
        in_specs=[smem_spec()] * 3 + [any_spec()] * (2 + len(first)),
        out_specs=vmem_spec() if far else any_spec(),
        scratch_shapes=([] if far else [pltpu.VMEM(shape, BF16)])
        + [
            pltpu.VMEM((STEPS, SLOTS, 2, HD), BF16),
            pltpu.VMEM((Z, 16, HD), F32),
            pltpu.SemaphoreType.DMA((Z * MAXB,)),
            pltpu.SemaphoreType.DMA,
        ]
        + ([] if far else [pltpu.SemaphoreType.DMA((Z,))]),
        compiler_params=params(16),
        cost_estimate=pl.CostEstimate(flops=0, bytes_accessed=(128 if far else 1) << 20, transcendentals=0),
        name="pack_far" if far else "pack_near",
    )(in_hbm(table), in_hbm(blocks), in_hbm(moves), in_hbm(new_kv), in_hbm(kv_pages), *map(in_hbm, first))


def place_of(tp):
    chip = lax.div(tp, 2)
    return lax.rem(tp, 2), lax.div(chip, 4), lax.rem(chip, 4)


def block_of(x, y, k, parity):
    dx, dy = SHIFTS[k]
    return (lax.rem(x + dx, 2) * 4 + lax.rem(y + dy, 4)) * 2 + parity


def attend_kernel(tbl, blk, q_hbm, nkv, kv, w, send_a, send_b, heads, wb, kvb, fresh, qs, ks, sc, ob, q, kvsem, wsem, fsem, qsem):
    tp = lax.axis_index("tp")
    core, x, y = place_of(tp)
    qcopy = pltpu.make_async_copy(q_hbm, q, qsem)
    qcopy.start()
    fcopy = pltpu.make_async_copy(
        nkv.at[:, :, :, pl.ds(pl.multiple_of(lax.div(tp, 2) * HD, HD), HD)], fresh, fsem
    )
    fcopy.start()
    pools = [pltpu.make_async_copy(kv.at[:, i, 0], kvb.at[i], kvsem.at[i]) for i in range(2)]
    for copy in pools:
        copy.start()
    wcopy = pltpu.make_async_copy(w, wb, wsem)
    wcopy.start()
    qcopy.wait()
    for t in range(STEPS):
        for g in range(2):
            qs[pl.ds(t * 2 + g, SLOTS, stride=4), :] = q[t, :, g * HD:(g + 1) * HD].astype(F32)
    fcopy.wait()
    fr = fresh[...].astype(F32)
    for u in range(STEPS):
        for c in range(2):
            val = fr[u, :, c, :]
            for j in range(4):
                ks[u * 2 + c, pl.ds(j, SLOTS, stride=4), :] = val

    scaling = HD ** (-0.5)
    row_a = lax.broadcasted_iota(jnp.int32, (8, TOK), 0) < 4
    block_no = lax.div(lax.broadcasted_iota(jnp.int32, (8, TOK), 1), PAGE)

    def score_pair(p, carry):
        rows = pl.ds(pl.multiple_of(p * 8, 8), 8)
        q8 = qs[rows, :].astype(BF16)
        parts = []
        for h in range(2):
            keys = jnp.concatenate([kvb[0, tbl[b, 2 * p + h]] for b in range(MAXB)], axis=0)
            parts.append(lax.dot_general(q8, keys, (((1,), (1,)), ((), ())), preferred_element_type=F32))
        s8 = jnp.where(row_a, parts[0], parts[1]) * scaling
        count = jnp.where(row_a, blk[2 * p], blk[2 * p + 1])
        sc[rows, :] = jnp.where(block_no < count, s8, MASKED)
        return carry

    pools[0].wait()
    lax.fori_loop(0, SLOTS // 2, score_pair, 0, unroll=True)

    qa = qs[...]
    f0 = jnp.sum(qa * ks[0], axis=-1, keepdims=True) * scaling
    f1 = jnp.sum(qa * ks[2], axis=-1, keepdims=True) * scaling
    late = lax.rem(lax.broadcasted_iota(jnp.int32, (SLOTS * 4, 1), 0), 4) >= 2
    f1 = jnp.where(late, f1, MASKED)
    s = sc[...]
    top = jnp.maximum(jnp.max(s, axis=-1, keepdims=True), jnp.maximum(f0, f1))
    e = jnp.exp(s - top)
    e0 = jnp.exp(f0 - top)
    e1 = jnp.exp(f1 - top)
    total = jnp.sum(e, axis=-1, keepdims=True) + e0 + e1
    sc[...] = e / total
    w0 = (e0 / total).astype(BF16).astype(F32)
    w1 = (e1 / total).astype(BF16).astype(F32)
    ob[...] = w0 * ks[1] + w1 * ks[3]
    row_o = lax.broadcasted_iota(jnp.int32, (8, HD), 0) < 4

    def mix_pair(p, carry):
        rows = pl.ds(pl.multiple_of(p * 8, 8), 8)
        w8 = sc[rows, :].astype(BF16)
        parts = []
        for h in range(2):
            vals = jnp.concatenate([kvb[1, tbl[b, 2 * p + h]] for b in range(MAXB)], axis=0)
            parts.append(jnp.dot(w8, vals, preferred_element_type=F32))
        ob[rows, :] += jnp.where(row_o, parts[0], parts[1])
        return carry

    pools[1].wait()
    lax.fori_loop(0, SLOTS // 2, mix_pair, 0, unroll=True)

    for t in range(STEPS):
        for g in range(2):
            heads[t * SLOTS:(t + 1) * SLOTS, g * HD:(g + 1) * HD] = ob[
                pl.ds(t * 2 + g, SLOTS, stride=4), :
            ].astype(BF16)
    wcopy.wait()
    sends = [ref.at[k] for ref in (send_a, send_b) for k in range(4)]
    project(heads, wb, sends, x, y, 1 - core)


def project(heads, wb, outs, x, y, parity):
    rows = heads[...]
    for k in range(CHIPS):
        cols = pl.ds(pl.multiple_of(block_of(x, y, k, parity) * SHARE, SHARE), SHARE)
        outs[k][...] = jnp.dot(rows, wb[:, cols], preferred_element_type=F32).astype(outs[k].dtype)


def attend(table, blocks, query, new_kv, kv_pages, out_weight):
    return pl.pallas_call(
        attend_kernel,
        out_shape=(
            pltpu.VMEM((4, ROWS, SHARE), BF16),
            pltpu.VMEM((4, ROWS, SHARE), BF16),
            pltpu.VMEM((ROWS, 2 * HD), BF16),
            pltpu.VMEM((2 * HD, D), BF16),
        ),
        in_specs=[smem_spec()] * 2 + [any_spec()] * 4,
        out_specs=(vmem_spec(),) * 4,
        scratch_shapes=[
            pltpu.VMEM((2, PAGES, PAGE, HD), BF16),
            pltpu.VMEM((STEPS, SLOTS, 2, HD), BF16),
            pltpu.VMEM((SLOTS * 4, HD), F32),
            pltpu.VMEM((4, SLOTS * 4, HD), F32),
            pltpu.VMEM((SLOTS * 4, TOK), F32),
            pltpu.VMEM((SLOTS * 4, HD), F32),
            pltpu.VMEM((STEPS, SLOTS, 2 * HD), BF16),
            pltpu.SemaphoreType.DMA((2,)),
            pltpu.SemaphoreType.DMA,
            pltpu.SemaphoreType.DMA,
            pltpu.SemaphoreType.DMA,
        ],
        compiler_params=params(32),
        cost_estimate=pl.CostEstimate(flops=10**10, bytes_accessed=64 << 20, transcendentals=10**5),
        name="attend",
    )(in_hbm(table), in_hbm(blocks), in_hbm(query), in_hbm(new_kv), in_hbm(kv_pages), in_hbm(out_weight))


def own_kernel(heads, wb, got_a, got_b, *outs):
    core, x, y = place_of(lax.axis_index("tp"))
    rows = heads[...]
    for k in range(CHIPS):
        cols = pl.ds(pl.multiple_of(block_of(x, y, k, core) * SHARE, SHARE), SHARE)
        part = jnp.dot(rows, wb[:, cols], preferred_element_type=F32)
        part = part + (got_a, got_b)[k // 4][k % 4].astype(F32)
        outs[k // 2][k % 2] = part.astype(outs[k // 2].dtype)


def own(heads, wb, got_a, got_b):
    return pl.pallas_call(
        own_kernel,
        out_shape=tuple(pltpu.VMEM((2, ROWS, SHARE), F32 if dy == 0 else BF16) for dy in range(4)),
        in_specs=[vmem_spec()] * 4,
        out_specs=(vmem_spec(),) * 4,
        compiler_params=params(16),
        cost_estimate=pl.CostEstimate(flops=1, bytes_accessed=1, transcendentals=0),
        name="own",
    )(in_vmem(heads), in_vmem(wb), in_vmem(got_a), in_vmem(got_b))


def finish_kernel(gain, near_rows, far, far_other, into, *refs):
    blocks, (normed, arrived, tail, buf, sems, nsem) = refs[:8], refs[8:]
    core, x, y = place_of(lax.axis_index("tp"))
    side = lax.rem(lax.axis_index("inst"), 2)
    copies = half_copies(far_other, arrived, 1 - side, 1 - core, sems, 0)
    squares = jnp.zeros((ROWS, SHARE), F32)
    for ref in blocks:
        for dx in range(2):
            v = ref[dx].astype(F32)
            squares = squares + v * v
    scale = lax.rsqrt(jnp.sum(squares, axis=-1, keepdims=True) / D + EPSILON)
    for part in range(2):
        for k in range(CHIPS):
            block = block_of(x, y, k, core if part == 0 else 1 - core)
            at = pl.ds(pl.multiple_of(block * SHARE, SHARE), SHARE)
            v = blocks[part * 4 + k // 2][k % 2].astype(F32)
            buf[:, at] = (v * scale * gain[:, at].astype(F32)).astype(BF16)
            copy = pltpu.make_async_copy(buf.at[:, at], normed.at[:, at], nsem.at[part * CHIPS + k])
            copy.start()
            copies.append(copy)
    for z in range(Z):
        tail[2 * z + side] = near_rows[z].astype(BF16)
        tail[2 * z + 1 - side] = far[z, TOK:MSG].astype(F32)[0:4].astype(BF16)
    for copy in copies:
        copy.wait()


def finish(gain, near_rows, far, far_other, into, mine, other):
    return pl.pallas_call(
        finish_kernel,
        out_shape=(
            pltpu.HBM((ROWS, D), BF16),
            pltpu.HBM((INST, MAXB, 2, PAGE, HD), BF16),
            jax.ShapeDtypeStruct((INST, 4, HD), BF16),
        ),
        in_specs=[vmem_spec()] * 4 + [any_spec()] + [vmem_spec()] * 8,
        out_specs=(any_spec(), any_spec(), vmem_spec()),
        scratch_shapes=[
            pltpu.VMEM((ROWS, D), BF16),
            pltpu.SemaphoreType.DMA((Z * MAXB,)),
            pltpu.SemaphoreType.DMA((2 * CHIPS,)),
        ],
        input_output_aliases={4: 1},
        compiler_params=params(24),
        cost_estimate=pl.CostEstimate(flops=4 * ROWS * D, bytes_accessed=8 << 20, transcendentals=0),
        name="finish",
    )(gain.reshape(1, D), near_rows, far, far_other, into, *mine, *other)


def half_copies(src, out, way, half, sems, first):
    copies = []
    for z in range(Z):
        for b in range(MAXB):
            copies.append(
                pltpu.make_async_copy(
                    src.at[z, pl.ds(b * PAGE, PAGE)],
                    out.at[2 * z + way, b, half],
                    sems.at[first + z * MAXB + b],
                )
            )
            copies[-1].start()
    return copies


def place_near_kernel(mine, other, out, rows, sems):
    core = lax.rem(lax.axis_index("tp"), 2)
    side = lax.rem(lax.axis_index("inst"), 2)
    copies = half_copies(mine, out, side, core, sems, 0)
    copies += half_copies(other, out, side, 1 - core, sems, Z * MAXB)
    for z in range(Z):
        rows[z] = mine[z, TOK:MSG].astype(F32)[0:4]
    for copy in copies:
        copy.wait()


def place_near(mine, other):
    return pl.pallas_call(
        place_near_kernel,
        out_shape=(
            pltpu.HBM((INST, MAXB, 2, PAGE, HD), BF16),
            jax.ShapeDtypeStruct((Z, 4, HD), F32),
        ),
        in_specs=[vmem_spec()] * 2,
        out_specs=(any_spec(), vmem_spec()),
        scratch_shapes=[pltpu.SemaphoreType.DMA((2 * Z * MAXB,))],
        compiler_params=params(8),
        cost_estimate=pl.CostEstimate(flops=0, bytes_accessed=3 << 20, transcendentals=0),
        name="place_near",
    )(mine, other)


def place_far_kernel(src, into, out, sems):
    core = lax.rem(lax.axis_index("tp"), 2)
    side = lax.rem(lax.axis_index("inst"), 2)
    for copy in half_copies(src, out, 1 - side, core, sems, 0):
        copy.wait()


def place_far(src, into):
    return pl.pallas_call(
        place_far_kernel,
        out_shape=pltpu.HBM((INST, MAXB, 2, PAGE, HD), BF16),
        in_specs=[vmem_spec(), any_spec()],
        out_specs=any_spec(),
        scratch_shapes=[pltpu.SemaphoreType.DMA((Z * MAXB,))],
        input_output_aliases={1: 0},
        compiler_params=params(8),
        cost_estimate=pl.CostEstimate(flops=0, bytes_accessed=3 << 20, transcendentals=0),
        name="place_far",
    )(src, into)


def tp_perm(dx, dy, dc):
    return [
        (k, ((k // 8) ^ dx) * 8 + ((k // 2 % 4 + dy) % 4) * 2 + ((k % 2) ^ dc)) for k in range(16)
    ]


SWAP = tp_perm(0, 0, 1)
CROSS = tp_perm(1, 0, 0)
AROUND = (2, 1, 3)


Z_GROUPS = [[2 * z + side for z in range(Z)] for side in range(2)]
SIDES = [(k, k ^ 1) for k in range(INST)]


def along_z(x):
    return lax.all_to_all(x, "inst", 0, 0, tiled=True, axis_index_groups=Z_GROUPS)


def after(x, *values):
    return lax.optimization_barrier((x, *values))[0]


def local(query, new_kv, residual, kv_pages, block_table, blocks, moves, out_weight, norm_gain):
    table = block_table.T
    near = pack(False, table, blocks, moves, new_kv, kv_pages)
    far = lax.ppermute(pack(True, table, blocks, moves, new_kv, kv_pages, near), "inst", SIDES)
    near = along_z(near)

    *sends, heads, weight = attend(table, blocks, query, new_kv, kv_pages, out_weight)
    got = [lax.ppermute(send, "tp", SWAP) for send in sends]
    sums = own(heads, weight, *got)
    terms = [lax.ppermute(sums[dy], "tp", tp_perm(0, dy, 0)) for dy in AROUND]
    terms[0] = after(terms[0], near, far)
    far = along_z(after(far, sums[1]))
    total = sums[0]
    for term in terms:
        total = total + term.astype(F32)
    own_rows = residual.reshape(ROWS, SHARE).astype(F32)
    part = jnp.stack([own_rows + total[0], total[1]]).astype(BF16)
    cross = lax.ppermute(part, "tp", CROSS)
    pair = jnp.stack(
        [(part[dx].astype(F32) + cross[1 - dx].astype(F32)).astype(BF16) for dx in range(2)]
    )
    hidden = pair[0].reshape(STEPS, SLOTS, SHARE)
    mine = {0: pair}
    for dy in AROUND:
        mine[dy] = lax.ppermute(pair, "tp", tp_perm(0, 4 - dy, 0))
    mine = [mine[dy] for dy in range(4)]
    near = after(near, pair)
    arrived, rows = place_near(near, lax.ppermute(near, "tp", SWAP))
    mine[2], arrived, hidden = lax.optimization_barrier((mine[2], arrived, hidden))
    other = [lax.ppermute(block, "tp", SWAP) for block in mine]
    far = after(far, *mine, other[3], other[0])
    far_other = lax.ppermute(far, "tp", SWAP)
    arrived = place_far(far, arrived)
    normed, arrived, tail = finish(norm_gain, rows, far, far_other, arrived, mine, other)
    return (
        hidden,
        normed.reshape(STEPS, SLOTS, D),
        arrived.reshape(INST, MAXB, 2, 1, PAGE, HD),
        tail.reshape(INST, STEPS, 2, 1, HD),
    )


def solution(mesh):
    in_specs = (
        P(None, "inst", "tp"),
        P(None, "inst", None, None),
        P(None, "inst", "tp"),
        P("inst", None, "tp", None, None),
        P("inst", None),
        P("inst"),
        P("inst", None),
        P("tp", None),
        P(),
    )
    out_specs = (
        P(None, "inst", "tp"),
        P(None, "inst", None),
        P("inst", None, None, "tp", None, None),
        P("inst", None, None, "tp", None),
    )
    return jax.shard_map(local, mesh=mesh, in_specs=in_specs, out_specs=out_specs, check_vma=False)
```

```python
import functools

import jax
import jax.numpy as jnp
from jax import lax
from jax.experimental import pallas as pl
from jax.experimental.pallas import tpu as pltpu
from jax.sharding import PartitionSpec as P

F32 = jnp.float32
BF16 = jnp.bfloat16
EPSILON = 1e-05
MASKED = -1e30

SLOTS = 48
MAXB = 3
PAGE = 128
HD = 128
STEPS = 2
INST = 16
CHIPS = 8
ROWS = STEPS * SLOTS
D = 8192
SHARE = 512
PAGES = SLOTS * MAXB
TOK = MAXB * PAGE
MSG = TOK + 16
Z = 8
SHIFTS = [(dx, dy) for dy in range(4) for dx in range(2)]


def any_spec():
    return pl.BlockSpec(memory_space=pl.ANY)


def smem_spec():
    return pl.BlockSpec(memory_space=pltpu.SMEM)


def vmem_spec():
    return pl.BlockSpec(memory_space=pltpu.VMEM)


def in_hbm(x):
    return pltpu.with_memory_space_constraint(x, pltpu.HBM)


def in_vmem(x):
    return pltpu.with_memory_space_constraint(x, pltpu.VMEM)


def params(mib):
    return pltpu.CompilerParams(vmem_limit_bytes=mib << 20)


def pack_kernel(far, tbl, blk, mv, nkv, kv, *refs):
    if far:
        buf, fresh, stage, sems, fsem = refs[-5:]
    else:
        out, buf, fresh, stage, sems, fsem, osems = refs
    tp = lax.axis_index("tp")
    core = lax.rem(tp, 2)
    side = lax.rem(lax.axis_index("inst"), 2)
    slots = [mv[0, 2 * z + (1 - side if far else side)] for z in range(Z)]

    def page_copy(z, b, page):
        return pltpu.make_async_copy(
            kv.at[page, core, 0], buf.at[z, pl.ds(b * PAGE, PAGE)], sems.at[z * MAXB + b]
        )

    fcopy = pltpu.make_async_copy(
        nkv.at[:, :, :, pl.ds(pl.multiple_of(lax.div(tp, 2) * HD, HD), HD)], fresh, fsem
    )
    fcopy.start()
    for z, m in enumerate(slots):
        for b in range(MAXB):
            page_copy(z, b, tbl[b, m]).start()
    stage[...] = jnp.zeros_like(stage)
    fcopy.wait()
    for z, m in enumerate(slots):
        stage[z, 0:2] = fresh[0, m].astype(F32)
        stage[z, 2:4] = fresh[1, m].astype(F32)
    buf[:, TOK:MSG] = stage[...].astype(BF16)
    copies = []
    for z, m in enumerate(slots):
        count = blk[m]
        for b in range(MAXB):
            page_copy(z, b, 0).wait()
            if b > 0:
                @pl.when(b >= count)
                def _():
                    buf[z, b * PAGE:(b + 1) * PAGE] = jnp.zeros((PAGE, HD), BF16)
        if not far:
            copies.append(pltpu.make_async_copy(buf.at[z], out.at[z], osems.at[z]))
            copies[-1].start()
    for copy in copies:
        copy.wait()


def pack(far, table, blocks, moves, new_kv, kv_pages, *first):
    shape = (Z, MSG, HD)
    return pl.pallas_call(
        functools.partial(pack_kernel, far),
        out_shape=pltpu.VMEM(shape, BF16) if far else pltpu.HBM(shape, BF16),
        in_specs=[smem_spec()] * 3 + [any_spec()] * (2 + len(first)),
        out_specs=vmem_spec() if far else any_spec(),
        scratch_shapes=([] if far else [pltpu.VMEM(shape, BF16)])
        + [
            pltpu.VMEM((STEPS, SLOTS, 2, HD), BF16),
            pltpu.VMEM((Z, 16, HD), F32),
            pltpu.SemaphoreType.DMA((Z * MAXB,)),
            pltpu.SemaphoreType.DMA,
        ]
        + ([] if far else [pltpu.SemaphoreType.DMA((Z,))]),
        compiler_params=params(16),
        cost_estimate=pl.CostEstimate(flops=0, bytes_accessed=(128 if far else 1) << 20, transcendentals=0),
        name="pack_far" if far else "pack_near",
    )(in_hbm(table), in_hbm(blocks), in_hbm(moves), in_hbm(new_kv), in_hbm(kv_pages), *map(in_hbm, first))


def place_of(tp):
    chip = lax.div(tp, 2)
    return lax.rem(tp, 2), lax.div(chip, 4), lax.rem(chip, 4)


def block_of(x, y, k, parity):
    dx, dy = SHIFTS[k]
    return (lax.rem(x + dx, 2) * 4 + lax.rem(y + dy, 4)) * 2 + parity


def attend_kernel(tbl, blk, q_hbm, nkv, kv, w, send_a, send_b, heads, wb, kvb, fresh, qs, ks, sc, ob, q, kvsem, wsem, fsem, qsem):
    tp = lax.axis_index("tp")
    core, x, y = place_of(tp)
    qcopy = pltpu.make_async_copy(q_hbm, q, qsem)
    qcopy.start()
    fcopy = pltpu.make_async_copy(
        nkv.at[:, :, :, pl.ds(pl.multiple_of(lax.div(tp, 2) * HD, HD), HD)], fresh, fsem
    )
    fcopy.start()
    pools = [pltpu.make_async_copy(kv.at[:, i, 0], kvb.at[i], kvsem.at[i]) for i in range(2)]
    for copy in pools:
        copy.start()
    wcopy = pltpu.make_async_copy(w, wb, wsem)
    wcopy.start()
    qcopy.wait()
    for t in range(STEPS):
        for g in range(2):
            qs[pl.ds(t * 2 + g, SLOTS, stride=4), :] = q[t, :, g * HD:(g + 1) * HD].astype(F32)
    fcopy.wait()
    fr = fresh[...].astype(F32)
    for u in range(STEPS):
        for c in range(2):
            val = fr[u, :, c, :]
            for j in range(4):
                ks[u * 2 + c, pl.ds(j, SLOTS, stride=4), :] = val

    scaling = HD ** (-0.5)
    row_a = lax.broadcasted_iota(jnp.int32, (8, TOK), 0) < 4
    block_no = lax.div(lax.broadcasted_iota(jnp.int32, (8, TOK), 1), PAGE)

    def score_pair(p, carry):
        rows = pl.ds(pl.multiple_of(p * 8, 8), 8)
        q8 = qs[rows, :].astype(BF16)
        parts = []
        for h in range(2):
            keys = jnp.concatenate([kvb[0, tbl[b, 2 * p + h]] for b in range(MAXB)], axis=0)
            parts.append(lax.dot_general(q8, keys, (((1,), (1,)), ((), ())), preferred_element_type=F32))
        s8 = jnp.where(row_a, parts[0], parts[1]) * scaling
        count = jnp.where(row_a, blk[2 * p], blk[2 * p + 1])
        sc[rows, :] = jnp.where(block_no < count, s8, MASKED)
        return carry

    pools[0].wait()
    lax.fori_loop(0, SLOTS // 2, score_pair, 0, unroll=True)

    qa = qs[...]
    f0 = jnp.sum(qa * ks[0], axis=-1, keepdims=True) * scaling
    f1 = jnp.sum(qa * ks[2], axis=-1, keepdims=True) * scaling
    late = lax.rem(lax.broadcasted_iota(jnp.int32, (SLOTS * 4, 1), 0), 4) >= 2
    f1 = jnp.where(late, f1, MASKED)
    s = sc[...]
    top = jnp.maximum(jnp.max(s, axis=-1, keepdims=True), jnp.maximum(f0, f1))
    e = jnp.exp(s - top)
    e0 = jnp.exp(f0 - top)
    e1 = jnp.exp(f1 - top)
    total = jnp.sum(e, axis=-1, keepdims=True) + e0 + e1
    sc[...] = e / total
    w0 = (e0 / total).astype(BF16).astype(F32)
    w1 = (e1 / total).astype(BF16).astype(F32)
    ob[...] = w0 * ks[1] + w1 * ks[3]
    row_o = lax.broadcasted_iota(jnp.int32, (8, HD), 0) < 4

    def mix_pair(p, carry):
        rows = pl.ds(pl.multiple_of(p * 8, 8), 8)
        w8 = sc[rows, :].astype(BF16)
        parts = []
        for h in range(2):
            vals = jnp.concatenate([kvb[1, tbl[b, 2 * p + h]] for b in range(MAXB)], axis=0)
            parts.append(jnp.dot(w8, vals, preferred_element_type=F32))
        ob[rows, :] += jnp.where(row_o, parts[0], parts[1])
        return carry

    pools[1].wait()
    lax.fori_loop(0, SLOTS // 2, mix_pair, 0, unroll=True)

    for t in range(STEPS):
        for g in range(2):
            heads[t * SLOTS:(t + 1) * SLOTS, g * HD:(g + 1) * HD] = ob[
                pl.ds(t * 2 + g, SLOTS, stride=4), :
            ].astype(BF16)
    wcopy.wait()
    sends = [ref.at[k] for ref in (send_a, send_b) for k in range(4)]
    project(heads, wb, sends, x, y, 1 - core)


def project(heads, wb, outs, x, y, parity):
    rows = heads[...]
    for k in range(CHIPS):
        cols = pl.ds(pl.multiple_of(block_of(x, y, k, parity) * SHARE, SHARE), SHARE)
        outs[k][...] = jnp.dot(rows, wb[:, cols], preferred_element_type=F32).astype(outs[k].dtype)


def attend(table, blocks, query, new_kv, kv_pages, out_weight):
    return pl.pallas_call(
        attend_kernel,
        out_shape=(
            pltpu.VMEM((4, ROWS, SHARE), BF16),
            pltpu.VMEM((4, ROWS, SHARE), BF16),
            pltpu.VMEM((ROWS, 2 * HD), BF16),
            pltpu.VMEM((2 * HD, D), BF16),
        ),
        in_specs=[smem_spec()] * 2 + [any_spec()] * 4,
        out_specs=(vmem_spec(),) * 4,
        scratch_shapes=[
            pltpu.VMEM((2, PAGES, PAGE, HD), BF16),
            pltpu.VMEM((STEPS, SLOTS, 2, HD), BF16),
            pltpu.VMEM((SLOTS * 4, HD), F32),
            pltpu.VMEM((4, SLOTS * 4, HD), F32),
            pltpu.VMEM((SLOTS * 4, TOK), F32),
            pltpu.VMEM((SLOTS * 4, HD), F32),
            pltpu.VMEM((STEPS, SLOTS, 2 * HD), BF16),
            pltpu.SemaphoreType.DMA((2,)),
            pltpu.SemaphoreType.DMA,
            pltpu.SemaphoreType.DMA,
            pltpu.SemaphoreType.DMA,
        ],
        compiler_params=params(32),
        cost_estimate=pl.CostEstimate(flops=10**10, bytes_accessed=64 << 20, transcendentals=10**5),
        name="attend",
    )(in_hbm(table), in_hbm(blocks), in_hbm(query), in_hbm(new_kv), in_hbm(kv_pages), in_hbm(out_weight))


def own_kernel(heads, wb, got_a, got_b, *outs):
    core, x, y = place_of(lax.axis_index("tp"))
    rows = heads[...]
    for k in range(CHIPS):
        cols = pl.ds(pl.multiple_of(block_of(x, y, k, core) * SHARE, SHARE), SHARE)
        part = jnp.dot(rows, wb[:, cols], preferred_element_type=F32)
        part = part + (got_a, got_b)[k // 4][k % 4].astype(F32)
        outs[k // 2][k % 2] = part.astype(outs[k // 2].dtype)


def own(heads, wb, got_a, got_b):
    return pl.pallas_call(
        own_kernel,
        out_shape=tuple(pltpu.VMEM((2, ROWS, SHARE), F32 if dy == 0 else BF16) for dy in range(4)),
        in_specs=[vmem_spec()] * 4,
        out_specs=(vmem_spec(),) * 4,
        compiler_params=params(16),
        cost_estimate=pl.CostEstimate(flops=1, bytes_accessed=1, transcendentals=0),
        name="own",
    )(in_vmem(heads), in_vmem(wb), in_vmem(got_a), in_vmem(got_b))


EARLY = (0, 1, 2, 3, 4, 7)


def block_squares(refs):
    squares = jnp.zeros((ROWS, SHARE), F32)
    for ref in refs:
        for dx in range(2):
            v = ref[dx].astype(F32)
            squares = squares + v * v
    return squares


def finish_kernel(gain, early, near_rows, far, far_other, into, *refs):
    blocks, (normed, arrived, tail, buf, sems, nsem) = refs[:8], refs[8:]
    core, x, y = place_of(lax.axis_index("tp"))
    side = lax.rem(lax.axis_index("inst"), 2)
    copies = half_copies(far_other, arrived, 1 - side, 1 - core, sems, 0)
    squares = early[...] + block_squares([blocks[k] for k in range(8) if k not in EARLY])
    scale = lax.rsqrt(jnp.sum(squares, axis=-1, keepdims=True) / D + EPSILON)
    for part in range(2):
        for k in range(CHIPS):
            block = block_of(x, y, k, core if part == 0 else 1 - core)
            at = pl.ds(pl.multiple_of(block * SHARE, SHARE), SHARE)
            v = blocks[part * 4 + k // 2][k % 2].astype(F32)
            buf[:, at] = (v * scale * gain[:, at].astype(F32)).astype(BF16)
            copy = pltpu.make_async_copy(buf.at[:, at], normed.at[:, at], nsem.at[part * CHIPS + k])
            copy.start()
            copies.append(copy)
    for z in range(Z):
        tail[2 * z + side] = near_rows[z].astype(BF16)
        tail[2 * z + 1 - side] = far[z, TOK:MSG].astype(F32)[0:4].astype(BF16)
    for copy in copies:
        copy.wait()


def finish(gain, early, near_rows, far, far_other, into, mine, other):
    return pl.pallas_call(
        finish_kernel,
        out_shape=(
            pltpu.HBM((ROWS, D), BF16),
            pltpu.HBM((INST, MAXB, 2, PAGE, HD), BF16),
            jax.ShapeDtypeStruct((INST, 4, HD), BF16),
        ),
        in_specs=[vmem_spec()] * 5 + [any_spec()] + [vmem_spec()] * 8,
        out_specs=(any_spec(), any_spec(), vmem_spec()),
        scratch_shapes=[
            pltpu.VMEM((ROWS, D), BF16),
            pltpu.SemaphoreType.DMA((Z * MAXB,)),
            pltpu.SemaphoreType.DMA((2 * CHIPS,)),
        ],
        input_output_aliases={5: 1},
        compiler_params=params(24),
        cost_estimate=pl.CostEstimate(flops=4 * ROWS * D, bytes_accessed=8 << 20, transcendentals=0),
        name="finish",
    )(gain.reshape(1, D), early, near_rows, far, far_other, into, *mine, *other)


def half_copies(src, out, way, half, sems, first):
    copies = []
    for z in range(Z):
        for b in range(MAXB):
            copies.append(
                pltpu.make_async_copy(
                    src.at[z, pl.ds(b * PAGE, PAGE)],
                    out.at[2 * z + way, b, half],
                    sems.at[first + z * MAXB + b],
                )
            )
            copies[-1].start()
    return copies


def place_near_kernel(mine, other, out, rows, sems):
    core = lax.rem(lax.axis_index("tp"), 2)
    side = lax.rem(lax.axis_index("inst"), 2)
    copies = half_copies(mine, out, side, core, sems, 0)
    copies += half_copies(other, out, side, 1 - core, sems, Z * MAXB)
    for z in range(Z):
        rows[z] = mine[z, TOK:MSG].astype(F32)[0:4]
    for copy in copies:
        copy.wait()


def place_near(mine, other):
    return pl.pallas_call(
        place_near_kernel,
        out_shape=(
            pltpu.HBM((INST, MAXB, 2, PAGE, HD), BF16),
            jax.ShapeDtypeStruct((Z, 4, HD), F32),
        ),
        in_specs=[vmem_spec()] * 2,
        out_specs=(any_spec(), vmem_spec()),
        scratch_shapes=[pltpu.SemaphoreType.DMA((2 * Z * MAXB,))],
        compiler_params=params(8),
        cost_estimate=pl.CostEstimate(flops=0, bytes_accessed=3 << 20, transcendentals=0),
        name="place_near",
    )(mine, other)


def place_far_kernel(src, into, *refs):
    blocks, (out, early, sems) = refs[:-3], refs[-3:]
    core = lax.rem(lax.axis_index("tp"), 2)
    side = lax.rem(lax.axis_index("inst"), 2)
    copies = half_copies(src, out, 1 - side, core, sems, 0)
    early[...] = block_squares(blocks)
    for copy in copies:
        copy.wait()


def place_far(src, into, blocks):
    return pl.pallas_call(
        place_far_kernel,
        out_shape=(
            pltpu.HBM((INST, MAXB, 2, PAGE, HD), BF16),
            pltpu.VMEM((ROWS, SHARE), F32),
        ),
        in_specs=[vmem_spec(), any_spec()] + [vmem_spec()] * len(blocks),
        out_specs=(any_spec(), vmem_spec()),
        scratch_shapes=[pltpu.SemaphoreType.DMA((Z * MAXB,))],
        input_output_aliases={1: 0},
        compiler_params=params(8),
        cost_estimate=pl.CostEstimate(flops=0, bytes_accessed=3 << 20, transcendentals=0),
        name="place_far",
    )(src, into, *blocks)


def tp_perm(dx, dy, dc):
    return [
        (k, ((k // 8) ^ dx) * 8 + ((k // 2 % 4 + dy) % 4) * 2 + ((k % 2) ^ dc)) for k in range(16)
    ]


SWAP = tp_perm(0, 0, 1)
CROSS = tp_perm(1, 0, 0)
AROUND = (2, 1, 3)


Z_GROUPS = [[2 * z + side for z in range(Z)] for side in range(2)]
SIDES = [(k, k ^ 1) for k in range(INST)]


def along_z(x):
    return lax.all_to_all(x, "inst", 0, 0, tiled=True, axis_index_groups=Z_GROUPS)


def after(x, *values):
    return lax.optimization_barrier((x, *values))[0]


def local(query, new_kv, residual, kv_pages, block_table, blocks, moves, out_weight, norm_gain):
    table = block_table.T
    near = pack(False, table, blocks, moves, new_kv, kv_pages)
    far = lax.ppermute(pack(True, table, blocks, moves, new_kv, kv_pages, near), "inst", SIDES)
    near = along_z(near)

    *sends, heads, weight = attend(table, blocks, query, new_kv, kv_pages, out_weight)
    got = [lax.ppermute(send, "tp", SWAP) for send in sends]
    sums = own(heads, weight, *got)
    terms = [lax.ppermute(sums[dy], "tp", tp_perm(0, dy, 0)) for dy in AROUND]
    terms[0] = after(terms[0], near, far)
    far = along_z(after(far, sums[1]))
    total = sums[0]
    for term in terms:
        total = total + term.astype(F32)
    own_rows = residual.reshape(ROWS, SHARE).astype(F32)
    part = jnp.stack([own_rows + total[0], total[1]]).astype(BF16)
    cross = lax.ppermute(part, "tp", CROSS)
    pair = jnp.stack(
        [(part[dx].astype(F32) + cross[1 - dx].astype(F32)).astype(BF16) for dx in range(2)]
    )
    hidden = pair[0].reshape(STEPS, SLOTS, SHARE)
    mine = {0: pair}
    for dy in AROUND:
        mine[dy] = lax.ppermute(pair, "tp", tp_perm(0, 4 - dy, 0))
    mine = [mine[dy] for dy in range(4)]
    near = after(near, part)
    arrived, rows = place_near(near, lax.ppermute(near, "tp", SWAP))
    mine[2], arrived, hidden = lax.optimization_barrier((mine[2], arrived, hidden))
    other = [lax.ppermute(block, "tp", SWAP) for block in mine]
    far = after(far, *mine, other[3], other[0])
    far_other = lax.ppermute(far, "tp", SWAP)
    blocks = [*mine, *other]
    arrived, early = place_far(far, arrived, [blocks[k] for k in EARLY])
    normed, arrived, tail = finish(norm_gain, early, rows, far, far_other, arrived, mine, other)
    return (
        hidden,
        normed.reshape(STEPS, SLOTS, D),
        arrived.reshape(INST, MAXB, 2, 1, PAGE, HD),
        tail.reshape(INST, STEPS, 2, 1, HD),
    )


def solution(mesh):
    in_specs = (
        P(None, "inst", "tp"),
        P(None, "inst", None, None),
        P(None, "inst", "tp"),
        P("inst", None, "tp", None, None),
        P("inst", None),
        P("inst"),
        P("inst", None),
        P("tp", None),
        P(),
    )
    out_specs = (
        P(None, "inst", "tp"),
        P(None, "inst", None),
        P("inst", None, None, "tp", None, None),
        P("inst", None, None, "tp", None),
    )
    return jax.shard_map(local, mesh=mesh, in_specs=in_specs, out_specs=out_specs, check_vma=False)
```
